128 devices in a mesh: seq: 64 (over z, x, y), dp: 2 (over core).
Axes of the slice: x: 4, y: 4, z: 4, core: 2. Of those that a mesh axis runs over, the one named last changes fastest.
Arguments:
- queries: bfloat16 [262144, 128], P(('dp', 'seq')), parts along dimension 0, may hold values from -42 to 42
- keys: bfloat16 [262144, 128], P(('dp', 'seq')), parts along dimension 0, may hold values from -4 to 4
- values: bfloat16 [262144, 128], P(('dp', 'seq')), parts along dimension 0, may hold values from -6 to 6
- grad_out: bfloat16 [262144, 128], P(('dp', 'seq')), parts along dimension 0, may hold values from -6 to 6
- block_lists: int32 [2048, 30], P(('dp', 'seq')), parts along dimension 0, may hold values from 0 to 15, as said below
Outputs:
- attn_out: bfloat16 [262144, 128], P(('dp', 'seq')), parts along dimension 0
- grad_query: bfloat16 [262144, 128], P(('dp', 'seq')), parts along dimension 0
- grad_key: bfloat16 [262144, 128], P(('dp', 'seq')), parts along dimension 0
- grad_value: bfloat16 [262144, 128], P(('dp', 'seq')), parts along dimension 0
The draws below stay inside these ranges and needn't reach their ends.
There are 2 independent parts, one for each index of `dp`. The reference program is written for one: setup_inputs(seed, part) draws one part's arguments, and reference() takes and returns one part's arrays. A program takes and returns all parts, laid end to end along the dimension named above; each array names one. Nothing has to cross between parts.
Inputs may be any that keep to these rules, and one draw needn't show every extreme that they name: `block_lists`: the columns of band k and one side hold (16) / 2**k distinct local block numbers, each a multiple of 2**(k-1).
All inputs are finite; a program needn't handle non-finite values.
Results may differ from the reference program's by a relative error of at most 0.03.
Values may be sent and summed in bfloat16 or wider, within the bound.
No kernel may reach another device: no remote copies, remote signals or barrier semaphores. Data moves between devices by JAX's collectives and lax.ppermute only.
A program may use at most 192 MiB of HBM per device.

```python
import math
from functools import reduce
import jax
import jax.numpy as jnp
from jax import lax

HEAD = 128
BLOCK = 128
FAR = 4
TOK_DEV = 2048
TOKENS = 131072
N_SEQ = 64


def shared_keys(key):
    normal_part = jax.random.normal(jax.random.fold_in(key, 101), (TOKENS, HEAD), jnp.float32)
    base = jnp.clip(normal_part, -4.0, 4.0)
    return base


def draw_keys(key, part):
    base = shared_keys(key)
    return base.astype(jnp.bfloat16)


def draw_queries(key, part):
    key = jax.random.fold_in(key, 4)
    normal_part = jax.random.normal(jax.random.fold_in(key, 1), (TOKENS, HEAD), jnp.float32)
    own = 2.5 * jnp.clip(normal_part, -4.0, 4.0)
    return own.astype(jnp.bfloat16)


def draw_block_lists(key, part):
    key = jax.random.fold_in(key, 5)
    nblk = TOK_DEV // BLOCK
    rows = TOKENS // BLOCK
    pieces = []
    for band in range(1, FAR + 1):
        stride = 2 ** (band - 1)
        cand = nblk // stride
        sel = nblk >> band
        for side in range(2):
            sub = jax.random.fold_in(key, band * 2 + side)
            ranks = jax.random.randint(sub, (rows, cand), 0, 1 << 20) * cand + jnp.arange(cand)[None, :]
            order = jnp.argsort(ranks, axis=1, stable=True)[:, :sel]
            pieces.append((order * stride).astype(jnp.int32))
    return jnp.concatenate(pieces, axis=1)


def levels(key, dims, cuts, smallest, largest):
    def one(position, parts):
        draws = jax.random.uniform(jax.random.fold_in(jax.random.fold_in(key, 6), position), (parts,), jnp.float32, smallest / len(cuts), largest / len(cuts))
        return jnp.repeat(jnp.exp(draws), dims[position] // parts).reshape((-1,) + (1,) * (len(dims) - position - 1))

    gain = one(*cuts[0])
    for cut in cuts[1:]:
        gain = gain * one(*cut)
    return gain


def normal_values(own_key, extent, spread, limit, cuts=(), kind=jnp.bfloat16):
    entries = jax.random.normal(own_key, extent, jnp.float32) * spread
    if len(cuts) > 0:
        entries = levels(own_key, extent, cuts, -0.22, 0.18) * entries
    return jnp.clip(entries, min=-limit, max=limit).astype(kind)


def setup_inputs(seed: int = 0, part: int = 0) -> dict:
    arg_keys = jax.random.split(jax.random.key(seed), 6)
    part_keys = jax.random.split(jax.random.fold_in(arg_keys[5], part), 6)
    return {
        "queries": draw_queries(jax.random.fold_in(jax.random.fold_in(arg_keys[5], part), 71), part),
        "keys": draw_keys(jax.random.fold_in(jax.random.fold_in(arg_keys[5], part), 71), part),
        "values": normal_values(part_keys[2], (TOKENS, HEAD), 1.0, 6.0, ((0, 64),)),
        "grad_out": normal_values(part_keys[3], (TOKENS, HEAD), 1.0, 6.0, ((0, 64),)),
        "block_lists": draw_block_lists(jax.random.fold_in(jax.random.fold_in(arg_keys[5], part), 71), part),
    }


def band_plan(nblk):
    plan = []
    start = 0
    for band in range(1, FAR + 1):
        stride = 2 ** (band - 1)
        sel = nblk >> band
        for sign in (1, -1):
            plan.append((stride, sel, start, sign * stride))
            start += sel
    return plan

def score_terms(query_blocks, key_group, shared, scale):
    form = 'qrd,ncd->qrnc' if shared else 'qrd,qncd->qrnc'
    return scale * jnp.einsum(form, query_blocks.astype(jnp.float32), key_group.astype(jnp.float32))

def to_half(x):
    return lax.optimization_barrier(x.astype(jnp.bfloat16)).astype(jnp.float32)

def reference(queries, keys, values, grad_out, block_lists):
    nblk = TOK_DEV // BLOCK
    scale = 1.0 / math.sqrt(HEAD)
    shape = (N_SEQ, nblk, BLOCK, HEAD)
    query_all = queries.reshape(shape)
    key_all = keys.reshape(shape)
    value_all = values.reshape(shape)
    grad_all = grad_out.reshape(shape)
    list_all = block_lists.reshape(N_SEQ, nblk, block_lists.shape[1])
    plan = band_plan(nblk)

    def shard_step(carry, shard):
        key_acc, value_acc = carry
        query_now = query_all[shard]
        grad_now = grad_all[shard].astype(jnp.float32)
        groups = [(key_all[shard], value_all[shard], jnp.array(True), None, shard)]
        for stride, sel, start, by in plan:
            source = shard - by
            valid = jnp.logical_and(source >= 0, source < N_SEQ)
            clipped = jnp.clip(source, 0, N_SEQ - 1).astype(jnp.int32)
            picked = list_all[shard][:, start:start + sel].astype(jnp.int32)
            groups.append((key_all[clipped][picked], value_all[clipped][picked], valid, picked, clipped))
        highs = []
        totals = []
        for key_group, value_group, valid, picked, owner in groups:
            score = score_terms(query_now, key_group, picked is None, scale)
            top = lax.optimization_barrier(jnp.max(score, axis=(2, 3)))
            totals.append(lax.optimization_barrier(jnp.sum(jnp.exp(score - top[:, :, None, None]), axis=(2, 3))))
            highs.append(jnp.where(valid, top, -jnp.inf))
        peak = reduce(jnp.maximum, highs)
        total = reduce(jnp.add, [part * jnp.exp(high - peak) for part, high in zip(totals, highs)])
        lse = peak + jnp.log(total)
        acc = jnp.zeros((nblk, BLOCK, HEAD), jnp.float32)
        for key_group, value_group, valid, picked, owner in groups:
            score = score_terms(query_now, key_group, picked is None, scale)
            weight = to_half(jnp.where(valid, jnp.exp(score - lse[:, :, None, None]), 0.0))
            form = 'qrnc,ncd->qrd' if picked is None else 'qrnc,qncd->qrd'
            acc = acc + jnp.einsum(form, weight, value_group.astype(jnp.float32))
        out_now = acc.astype(jnp.bfloat16)
        delta = lax.optimization_barrier(jnp.sum(grad_now * out_now.astype(jnp.float32), axis=-1))
        dquery = jnp.zeros((nblk, BLOCK, HEAD), jnp.float32)
        query_f = query_now.astype(jnp.float32)
        for key_group, value_group, valid, picked, owner in groups:
            shared = picked is None
            score = score_terms(query_now, key_group, shared, scale)
            prob = jnp.where(valid, jnp.exp(score - lse[:, :, None, None]), 0.0)
            weight = to_half(prob)
            form = 'qrd,ncd->qrnc' if shared else 'qrd,qncd->qrnc'
            dweight = jnp.einsum(form, grad_now, value_group.astype(jnp.float32))
            dscore = to_half(prob * (dweight - delta[:, :, None, None]))
            back = 'qrnc,ncd->qrd' if shared else 'qrnc,qncd->qrd'
            dquery = dquery + jnp.einsum(back, dscore, key_group.astype(jnp.float32))
            if shared:
                key_acc = key_acc.at[shard].add(jnp.einsum('qrnc,qrd->ncd', dscore, query_f))
                value_acc = value_acc.at[shard].add(jnp.einsum('qrnc,qrd->ncd', weight, grad_now))
            else:
                part_key = jnp.einsum('qrnc,qrd->qncd', dscore, query_f)
                part_value = jnp.einsum('qrnc,qrd->qncd', weight, grad_now)
                key_acc = key_acc.at[owner, picked].add(jnp.where(valid, part_key, 0.0))
                value_acc = value_acc.at[owner, picked].add(jnp.where(valid, part_value, 0.0))
        dquery_out = (scale * dquery).astype(jnp.bfloat16)
        return ((key_acc, value_acc), (out_now, dquery_out))
    zeros = jnp.zeros(shape, jnp.float32)
    (key_acc, value_acc), (outs, dquery_all) = lax.scan(shard_step, (zeros, zeros), jnp.arange(N_SEQ, dtype=jnp.int32))
    attn_out = outs.reshape(TOKENS, HEAD)
    grad_query = dquery_all.reshape(TOKENS, HEAD)
    grad_key = (scale * key_acc).astype(jnp.bfloat16).reshape(TOKENS, HEAD)
    grad_value = value_acc.astype(jnp.bfloat16).reshape(TOKENS, HEAD)
    return (attn_out, grad_query, grad_key, grad_value)
```

```python
import functools
import math

import jax
import jax.numpy as jnp
from jax import lax
from jax.experimental import pallas as pl
from jax.experimental.pallas import tpu as pltpu
from jax.sharding import PartitionSpec as P

BLOCK = 128
HEAD = 128
NBLK = 16
FAR = 4
SCALE = 1.0 / math.sqrt(HEAD)
LOG2E = 1.4426950408889634
COEF = SCALE * LOG2E
BIG = 1e30
MIB = 2**20

SLOT_BLOCK = [0, 8, 4, 12, 2, 6, 10, 14, 1, 3, 5, 7, 9, 11, 13, 15]


def band_columns():
    plan = []
    start = 0
    for band in range(1, FAR + 1):
        stride = 2 ** (band - 1)
        sel = NBLK >> band
        for side, sign in enumerate((1, -1)):
            plan.append((band, side, start, sel, sign * stride))
            start += sel
    return plan


PLAN = band_columns()


def nt(a, b):
    return lax.dot_general(a, b, (((1,), (1,)), ((), ())), preferred_element_type=jnp.float32)


def nn(a, b):
    return lax.dot_general(a, b, (((1,), (0,)), ((), ())), preferred_element_type=jnp.float32)


def tn(a, b):
    return lax.dot_general(a, b, (((0,), (0,)), ((), ())), preferred_element_type=jnp.float32)


def shift(value, by):
    count = lax.axis_size("seq")
    first, last = max(0, -by), min(count, count - by)
    return lax.ppermute(value, "seq", [(s, s + by) for s in range(first, last)])


def params(limit=40):
    return pltpu.CompilerParams(vmem_limit_bytes=limit * MIB)


VMEM = pl.BlockSpec(memory_space=pltpu.VMEM)
SMEM = pl.BlockSpec(memory_space=pltpu.SMEM)


def cost(pairs, products, exps, moved):
    return pl.CostEstimate(
        flops=2 * pairs * products * BLOCK * BLOCK * HEAD,
        transcendentals=exps * pairs * BLOCK * BLOCK,
        bytes_accessed=moved,
    )


def pack_kernel(k_ref, v_ref, out_ref):
    for slot, block in enumerate(SLOT_BLOCK):
        out_ref[slot, 0] = k_ref[block]
        out_ref[slot, 1] = v_ref[block]


def pack(key_blocks, value_blocks):
    return pl.pallas_call(
        pack_kernel,
        out_shape=jax.ShapeDtypeStruct((NBLK, 2, BLOCK, HEAD), jnp.bfloat16),
        in_specs=[VMEM, VMEM],
        out_specs=VMEM,
        name="pack",
    )(key_blocks, value_blocks)


def lane_all(x):
    return jnp.broadcast_to(x, (x.shape[0], 128))


def two(ref, a, b, which):
    return jnp.concatenate((ref[a, which], ref[b, which]), axis=0)


def entries_of(group):
    entries = []
    for n, (band, side, start, sel, by) in enumerate(group):
        for c in range(sel):
            entries.append((n, start + c))
    return entries


def forward_local_kernel(q_ref, k_ref, v_ref, m_ref, l_ref, acc_ref, s_ref):
    width = NBLK * BLOCK

    def step(i, carry):
        s = nt(q_ref[i], k_ref[...].reshape(width, HEAD))
        s_ref[...] = s
        top = s[:, :128]
        for j in range(1, NBLK):
            top = jnp.maximum(top, s[:, j * 128 : (j + 1) * 128])
        m = lane_all(jnp.max(top, axis=1, keepdims=True))
        total = jnp.zeros((BLOCK, 128), jnp.float32)
        acc = jnp.zeros((BLOCK, HEAD), jnp.float32)
        for j in range(0, NBLK, 2):
            parts = []
            for h in (j, j + 1):
                p = jnp.exp2((s_ref[:, h * 128 : (h + 1) * 128] - m) * COEF)
                total += p
                parts.append(p.astype(jnp.bfloat16))
            acc += nn(
                jnp.concatenate(parts, axis=1), v_ref[j : j + 2].reshape(2 * BLOCK, HEAD)
            )
        m_ref[i] = m
        l_ref[i] = total
        acc_ref[i] = acc
        return carry

    lax.fori_loop(0, NBLK, step, 0)


STAT = jax.ShapeDtypeStruct((NBLK, BLOCK, 128), jnp.float32)
HALF = jax.ShapeDtypeStruct((NBLK, BLOCK, HEAD), jnp.bfloat16)


def forward_local(q, k, v):
    return pl.pallas_call(
        forward_local_kernel,
        out_shape=(STAT, STAT, STAT),
        in_specs=[VMEM] * 3,
        out_specs=(VMEM,) * 3,
        scratch_shapes=[pltpu.VMEM((BLOCK, NBLK * BLOCK), jnp.float32)],
        compiler_params=params(),
        cost_estimate=cost(256, 2, 1, 5 * MIB),
        name="forward_local",
    )(q, k, v)


def forward_far_kernel(group, last, *refs):
    count = len(group)
    slots, bias, q_ref, mi_ref, li_ref, acci_ref = refs[:6]
    kv = refs[6 : 6 + count]
    rest = refs[6 + count :]
    if last:
        g_ref, out_ref, lse_ref, delta_ref, s_ref = rest
    else:
        m_ref, l_ref, acc_ref, s_ref = rest
    entries = entries_of(group)

    def step(i, carry):
        q = q_ref[i]
        tops = [None] * count
        for e in range(0, len(entries), 2):
            (na, ca), (nb, cb) = entries[e], entries[e + 1]
            keys = jnp.concatenate((kv[na][slots[i, ca], 0], kv[nb][slots[i, cb], 0]), axis=0)
            s = nt(q, keys)
            s_ref[:, e * 128 : (e + 2) * 128] = s
            for n, half in ((na, s[:, :128]), (nb, s[:, 128:])):
                tops[n] = half if tops[n] is None else jnp.maximum(tops[n], half)
        top = tops[0] - bias[group[0][0] * 2 + group[0][1]]
        for n in range(1, count):
            top = jnp.maximum(top, tops[n] - bias[group[n][0] * 2 + group[n][1]])
        before = mi_ref[i]
        m = jnp.maximum(before, lane_all(jnp.max(top, axis=1, keepdims=True)))
        keep = jnp.exp2((before - m) * COEF)
        total = li_ref[i] * keep
        acc = acci_ref[i] * keep
        offsets = [m + bias[band * 2 + side] for band, side, _, _, _ in group]
        for e in range(0, len(entries), 2):
            parts = []
            for h in (e, e + 1):
                p = jnp.exp2((s_ref[:, h * 128 : (h + 1) * 128] - offsets[entries[h][0]]) * COEF)
                total += p
                parts.append(p.astype(jnp.bfloat16))
            (na, ca), (nb, cb) = entries[e], entries[e + 1]
            vals = jnp.concatenate((kv[na][slots[i, ca], 1], kv[nb][slots[i, cb], 1]), axis=0)
            acc += nn(jnp.concatenate(parts, axis=1), vals)
        if last:
            full = lane_all(jnp.sum(total, axis=1, keepdims=True))
            out = (acc / full).astype(jnp.bfloat16)
            out_ref[i] = out
            lse_ref[i] = m * COEF + jnp.log2(full)
            delta = jnp.sum(
                g_ref[i].astype(jnp.float32) * out.astype(jnp.float32), axis=1, keepdims=True
            )
            delta_ref[i] = lane_all(delta)
        else:
            m_ref[i] = m
            l_ref[i] = total
            acc_ref[i] = acc
        return carry

    lax.fori_loop(0, NBLK, step, 0)


def forward_far(group, last, slots, bias, q, stats, kv, grad):
    entries = entries_of(group)
    extra = (grad,) if last else ()
    outs = (HALF, STAT, STAT) if last else (STAT, STAT, STAT)
    return pl.pallas_call(
        functools.partial(forward_far_kernel, group, last),
        out_shape=outs,
        in_specs=[SMEM, SMEM] + [VMEM] * (4 + len(kv) + len(extra)),
        out_specs=(VMEM,) * 3,
        scratch_shapes=[pltpu.VMEM((BLOCK, len(entries) * BLOCK), jnp.float32)],
        compiler_params=params(),
        cost_estimate=cost(16 * len(entries), 2, 1, 8 * MIB),
        name="forward_far",
    )(slots, bias, q, *stats, *kv, *extra)


def backward_pair(q, g, lse_a, lse_b, delta, keys, vals):
    s = nt(q, keys)
    dp = nt(g, vals)
    probs = []
    dss = []
    for h, lse in ((0, lse_a), (1, lse_b)):
        p = jnp.exp2(s[:, h * 128 : (h + 1) * 128] * COEF - lse)
        ds = p * (dp[:, h * 128 : (h + 1) * 128] - delta)
        probs.append(p.astype(jnp.bfloat16))
        dss.append(ds.astype(jnp.bfloat16))
    return jnp.concatenate(probs, axis=1), jnp.concatenate(dss, axis=1)


def backward_far_kernel(group, first, *refs):
    count = len(group)
    slots, bias, q_ref, g_ref, lse_ref, delta_ref = refs[:6]
    kv = refs[6 : 6 + count]
    rest = refs[6 + count :]
    if not first:
        dqi_ref, rest = rest[0], rest[1:]
    dq_ref, part, acc = rest[0], rest[1 : 1 + count], rest[1 + count :]
    entries = entries_of(group)
    for a in acc:
        a[...] = jnp.zeros_like(a)

    def step(i, carry):
        q = q_ref[i]
        g = g_ref[i]
        lse = lse_ref[i]
        delta = delta_ref[i]
        offsets = [lse + bias[band * 2 + side] for band, side, _, _, _ in group]
        dq = jnp.zeros((BLOCK, HEAD), jnp.float32) if first else dqi_ref[i]
        for e in range(0, len(entries), 2):
            (na, ca), (nb, cb) = entries[e], entries[e + 1]
            sa, sb = slots[i, ca], slots[i, cb]
            keys = jnp.concatenate((kv[na][sa, 0], kv[nb][sb, 0]), axis=0)
            vals = jnp.concatenate((kv[na][sa, 1], kv[nb][sb, 1]), axis=0)
            p, ds = backward_pair(q, g, offsets[na], offsets[nb], delta, keys, vals)
            dq += nn(ds, keys)
            dk = tn(ds, q)
            dv = tn(p, g)
            acc[na][sa, 0] += dk[:BLOCK]
            acc[na][sa, 1] += dv[:BLOCK]
            acc[nb][sb, 0] += dk[BLOCK:]
            acc[nb][sb, 1] += dv[BLOCK:]
        dq_ref[i] = dq
        return carry

    lax.fori_loop(0, NBLK, step, 0)
    for out, a in zip(part, acc):
        out[...] = a[...].astype(jnp.bfloat16)


def backward_far(group, slots, bias, q, g, lse, delta, kv, dq):
    entries = entries_of(group)
    extra = () if dq is None else (dq,)
    return pl.pallas_call(
        functools.partial(backward_far_kernel, group, dq is None),
        out_shape=(STAT,) + tuple(jax.ShapeDtypeStruct(x.shape, jnp.bfloat16) for x in kv),
        in_specs=[SMEM, SMEM] + [VMEM] * (4 + len(kv) + len(extra)),
        out_specs=(VMEM,) * (1 + len(kv)),
        scratch_shapes=[pltpu.VMEM(x.shape, jnp.float32) for x in kv],
        compiler_params=params(),
        cost_estimate=cost(16 * len(entries), 5, 1, 8 * MIB),
        name="backward_far",
    )(slots, bias, q, g, lse, delta, *kv, *extra)


def backward_local_kernel(
    q_ref, g_ref, lse_ref, delta_ref, k_ref, v_ref, dqi_ref, dq_ref, dk_ref, dv_ref
):
    dk_ref[...] = jnp.zeros_like(dk_ref)
    dv_ref[...] = jnp.zeros_like(dv_ref)

    def step(i, carry):
        q = q_ref[i]
        g = g_ref[i]
        lse = lse_ref[i]
        delta = delta_ref[i]
        dq = dqi_ref[i]
        for j in range(0, NBLK, 2):
            keys = k_ref[j : j + 2].reshape(2 * BLOCK, HEAD)
            vals = v_ref[j : j + 2].reshape(2 * BLOCK, HEAD)
            p, ds = backward_pair(q, g, lse, lse, delta, keys, vals)
            dq += nn(ds, keys)
            dk_ref[j : j + 2] += tn(ds, q).reshape(2, BLOCK, HEAD)
            dv_ref[j : j + 2] += tn(p, g).reshape(2, BLOCK, HEAD)
        dq_ref[i] = (dq * SCALE).astype(jnp.bfloat16)
        return carry

    lax.fori_loop(0, NBLK, step, 0)


def backward_local(q, g, lse, delta, k, v, dq):
    return pl.pallas_call(
        backward_local_kernel,
        out_shape=(HALF, STAT, STAT),
        in_specs=[VMEM] * 7,
        out_specs=(VMEM,) * 3,
        compiler_params=params(),
        cost_estimate=cost(256, 5, 1, 8 * MIB),
        name="backward_local",
    )(q, g, lse, delta, k, v, dq)


def finish_kernel(dk_ref, dv_ref, *refs):
    parts, (gk_ref, gv_ref) = refs[:-2], refs[-2:]
    for slot, block in enumerate(SLOT_BLOCK):
        dk = dk_ref[block]
        dv = dv_ref[block]
        for part in parts:
            if slot < part.shape[0]:
                dk += part[slot, 0].astype(jnp.float32)
                dv += part[slot, 1].astype(jnp.float32)
        gk_ref[block] = (dk * SCALE).astype(jnp.bfloat16)
        gv_ref[block] = dv.astype(jnp.bfloat16)


def finish(dk, dv, parts):
    return pl.pallas_call(
        finish_kernel,
        out_shape=(HALF, HALF),
        in_specs=[VMEM] * (2 + len(parts)),
        out_specs=(VMEM,) * 2,
        compiler_params=params(),
        name="finish",
    )(dk, dv, *parts)


def slot_of(block):
    return jnp.where(
        block % 2 == 1,
        8 + block // 2,
        jnp.where(
            block % 4 == 2, 4 + block // 4, jnp.where(block % 8 == 4, 2 + block // 8, block // 8)
        ),
    )


FORWARD_GROUPS = ((1, 3, 4), (2,))
BACKWARD_GROUPS = ((2,), (3, 4), (1,))


def local(queries, keys, values, grad_out, block_lists):
    shape = (NBLK, BLOCK, HEAD)
    q, k, v, g = (x.reshape(shape) for x in (queries, keys, values, grad_out))
    position = lax.axis_index("seq")
    devices = lax.axis_size("seq")
    slots = slot_of(block_lists)
    biases = [jnp.float32(0.0)] * 2
    for band, side, start, sel, by in PLAN:
        source = position - by
        valid = jnp.logical_and(source >= 0, source < devices)
        biases.append(jnp.where(valid, 0.0, BIG).astype(jnp.float32))
    bias = jnp.stack(biases)
    packed = pack(k, v)
    fetched = {}
    for entry in sorted(PLAN, key=lambda e: -e[0]):
        band, side, start, sel, by = entry
        fetched[band, side] = shift(packed[: NBLK >> (band - 1)], by)
    stats = forward_local(q, k, v)
    for n, bands in enumerate(FORWARD_GROUPS):
        group = [e for e in PLAN if e[0] in bands]
        last = n == len(FORWARD_GROUPS) - 1
        kv = [fetched[e[0], e[1]] for e in group]
        stats = forward_far(group, last, slots, bias, q, stats, kv, g)
    out, lse, delta = stats
    dq = None
    returned = []
    for bands in BACKWARD_GROUPS:
        group = [e for e in PLAN if e[0] in bands]
        kv = [fetched[e[0], e[1]] for e in group]
        dq, *parts = backward_far(group, slots, bias, q, g, lse, delta, kv, dq)
        for (band, side, start, sel, by), part in zip(group, parts):
            returned.append(shift(part, -by))
    dq, dk, dv = backward_local(q, g, lse, delta, k, v, dq)
    gk, gv = finish(dk, dv, returned)
    flat = (NBLK * BLOCK, HEAD)
    return tuple(x.reshape(flat) for x in (out, dq, gk, gv))


def solution(mesh):
    spec = P(("dp", "seq"), None)
    return jax.shard_map(
        local,
        mesh=mesh,
        in_specs=(spec,) * 5,
        out_specs=(spec,) * 4,
        check_vma=False,
    )
```

```python
import functools
import math

import jax
import jax.numpy as jnp
from jax import lax
from jax.experimental import pallas as pl
from jax.experimental.pallas import tpu as pltpu
from jax.sharding import PartitionSpec as P

BLOCK = 128
HEAD = 128
NBLK = 16
FAR = 4
SCALE = 1.0 / math.sqrt(HEAD)
LOG2E = 1.4426950408889634
COEF = SCALE * LOG2E
BIG = 1e30
MIB = 2**20

SLOT_BLOCK = [0, 8, 4, 12, 2, 6, 10, 14, 1, 3, 5, 7, 9, 11, 13, 15]


def band_columns():
    plan = []
    start = 0
    for band in range(1, FAR + 1):
        stride = 2 ** (band - 1)
        sel = NBLK >> band
        for side, sign in enumerate((1, -1)):
            plan.append((band, side, start, sel, sign * stride))
            start += sel
    return plan


PLAN = band_columns()


def nt(a, b):
    return lax.dot_general(a, b, (((1,), (1,)), ((), ())), preferred_element_type=jnp.float32)


def nn(a, b):
    return lax.dot_general(a, b, (((1,), (0,)), ((), ())), preferred_element_type=jnp.float32)


def tn(a, b):
    return lax.dot_general(a, b, (((0,), (0,)), ((), ())), preferred_element_type=jnp.float32)


def shift(value, by):
    count = lax.axis_size("seq")
    first, last = max(0, -by), min(count, count - by)
    return lax.ppermute(value, "seq", [(s, s + by) for s in range(first, last)])


def params(limit=16):
    return pltpu.CompilerParams(vmem_limit_bytes=limit * MIB)


VMEM = pl.BlockSpec(memory_space=pltpu.VMEM)
SMEM = pl.BlockSpec(memory_space=pltpu.SMEM)


def cost(pairs, products, exps, moved):
    return pl.CostEstimate(
        flops=2 * pairs * products * BLOCK * BLOCK * HEAD,
        transcendentals=exps * pairs * BLOCK * BLOCK,
        bytes_accessed=moved,
    )


def slot_of(own):
    return jnp.where(
        (own & 1) == 1,
        8 + (own >> 1),
        jnp.where(
            (own & 3) == 2, 4 + (own >> 2), jnp.where((own & 7) == 4, 2 + (own >> 3), own >> 3)
        ),
    )


def pack_kernel(k_ref, v_ref, lists_ref, slots_ref, *outs):
    slots_ref[...] = slot_of(lists_ref[...])
    for slot, own in enumerate(SLOT_BLOCK):
        for out in outs:
            if slot < out.shape[0]:
                out[slot, 0] = k_ref[own]
                out[slot, 1] = v_ref[own]


def pack(key_blocks, value_blocks, lists, *sizes):
    return pl.pallas_call(
        pack_kernel,
        out_shape=(jax.ShapeDtypeStruct(lists.shape, jnp.int32),)
        + tuple(jax.ShapeDtypeStruct((n, 2, BLOCK, HEAD), jnp.bfloat16) for n in sizes),
        in_specs=[VMEM] * 3,
        out_specs=(VMEM,) * (1 + len(sizes)),
        compiler_params=params(),
        name="pack",
    )(key_blocks, value_blocks, lists)


def hand_on_kernel(a_ref, b_ref, out_a_ref, out_b_ref):
    out_a_ref[...] = a_ref[: NBLK // 2]
    out_b_ref[...] = b_ref[: NBLK // 2]


def hand_on(a, b):
    half = jax.ShapeDtypeStruct((NBLK // 2, 2, BLOCK, HEAD), jnp.bfloat16)
    return pl.pallas_call(
        hand_on_kernel,
        out_shape=(half, half),
        in_specs=[VMEM] * 2,
        out_specs=(VMEM,) * 2,
        compiler_params=params(),
        name="hand_on",
    )(a, b)


def merge_kernel(*refs):
    count = len(refs) // 3
    for base, more, out in zip(refs[:count], refs[count : 2 * count], refs[2 * count :]):
        half = more.shape[0]
        total = base[:half].astype(jnp.float32) + more[...].astype(jnp.float32)
        out[:half] = total.astype(jnp.bfloat16)
        out[half:] = base[half:]


def merge(bases, mores):
    return pl.pallas_call(
        merge_kernel,
        out_shape=tuple(jax.ShapeDtypeStruct(x.shape, x.dtype) for x in bases),
        in_specs=[VMEM] * (2 * len(bases)),
        out_specs=(VMEM,) * len(bases),
        compiler_params=params(),
        name="merge",
    )(*bases, *mores)


def lane_all(x):
    return jnp.broadcast_to(x, (x.shape[0], 128))


def entries_of(group):
    return [
        (n, start + c) for n, (band, side, start, sel, by) in enumerate(group) for c in range(sel)
    ]


def gather(kv, entries, slots, i, which):
    return jnp.concatenate([kv[n][slots[i, c], which] for n, c in entries], axis=0)


def block(e):
    return slice(e * BLOCK, (e + 1) * BLOCK)


def bias_of(bias, entry):
    return bias[entry[0] * 2 + entry[1]]


STAT = jax.ShapeDtypeStruct((NBLK, BLOCK, 128), jnp.float32)
HALF = jax.ShapeDtypeStruct((NBLK, BLOCK, HEAD), jnp.bfloat16)
UNROLL = 4


def staggered(stages, copies=UNROLL):
    for tick in range(copies + len(stages) - 1):
        for n, stage in enumerate(stages):
            if 0 <= tick - n < copies:
                stage(tick - n)


def forward_local_kernel(q_ref, k_ref, v_ref, m_ref, l_ref, acc_ref, *scratch):
    width = NBLK * BLOCK

    def step(t, carry):
        def scores(u):
            scratch[2 * u][...] = nt(q_ref[t * UNROLL + u], k_ref[...].reshape(width, HEAD))

        def weights(u):
            s_ref, p_ref = scratch[2 * u : 2 * u + 2]
            top = s_ref[:, block(0)]
            for e in range(1, NBLK):
                top = jnp.maximum(top, s_ref[:, block(e)])
            m = lane_all(jnp.max(top, axis=1, keepdims=True))
            m_ref[t * UNROLL + u] = m
            total = jnp.zeros((BLOCK, 128), jnp.float32)
            for e in range(NBLK):
                p = jnp.exp2((s_ref[:, block(e)] - m) * COEF)
                total += p
                p_ref[:, block(e)] = p.astype(jnp.bfloat16)
            l_ref[t * UNROLL + u] = total

        def sums(u):
            acc_ref[t * UNROLL + u] = nn(scratch[2 * u + 1][...], v_ref[...].reshape(width, HEAD))

        staggered((scores, weights, sums))
        return carry

    lax.fori_loop(0, NBLK // UNROLL, step, 0)


def forward_scratch(width):
    return [
        pltpu.VMEM((BLOCK, width), jnp.float32),
        pltpu.VMEM((BLOCK, width), jnp.bfloat16),
    ] * UNROLL


def forward_local(q, k, v):
    return pl.pallas_call(
        forward_local_kernel,
        out_shape=(STAT, STAT, STAT),
        in_specs=[VMEM] * 3,
        out_specs=(VMEM,) * 3,
        scratch_shapes=forward_scratch(NBLK * BLOCK),
        compiler_params=params(),
        cost_estimate=cost(256, 2, 1, 5 * MIB),
        name="forward_local",
    )(q, k, v)


def forward_far_kernel(group, last, *refs):
    count = len(group)
    slots, bias, q_ref, mi_ref, li_ref, acci_ref = refs[:6]
    kv = refs[6 : 6 + count]
    rest = refs[6 + count :]
    if last:
        g_ref, out_ref, lse_ref, delta_ref = rest[:4]
        scratch = rest[4:]
    else:
        m_ref, l_ref, acc_ref = rest[:3]
        scratch = rest[3:]
    entries = entries_of(group)

    def step(t, carry):
        highs = [None] * UNROLL
        totals = [None] * UNROLL

        def scores(u):
            i = t * UNROLL + u
            scratch[2 * u][...] = nt(q_ref[i], gather(kv, entries, slots, i, 0))

        def weights(u):
            i = t * UNROLL + u
            s_ref, p_ref = scratch[2 * u : 2 * u + 2]
            top = None
            for n in range(count):
                own = [e for e in range(len(entries)) if entries[e][0] == n]
                part = s_ref[:, block(own[0])]
                for e in own[1:]:
                    part = jnp.maximum(part, s_ref[:, block(e)])
                part = part - bias_of(bias, group[n])
                top = part if top is None else jnp.maximum(top, part)
            m = jnp.maximum(mi_ref[i], lane_all(jnp.max(top, axis=1, keepdims=True)))
            total = li_ref[i] * jnp.exp2((mi_ref[i] - m) * COEF)
            offsets = [m + bias_of(bias, entry) for entry in group]
            for e, (n, c) in enumerate(entries):
                p = jnp.exp2((s_ref[:, block(e)] - offsets[n]) * COEF)
                total += p
                p_ref[:, block(e)] = p.astype(jnp.bfloat16)
            highs[u] = m
            totals[u] = total

        def sums(u):
            i = t * UNROLL + u
            m = highs[u]
            acc = acci_ref[i] * jnp.exp2((mi_ref[i] - m) * COEF)
            acc += nn(scratch[2 * u + 1][...], gather(kv, entries, slots, i, 1))
            if last:
                full = lane_all(jnp.sum(totals[u], axis=1, keepdims=True))
                out = (acc / full).astype(jnp.bfloat16)
                out_ref[i] = out
                lse_ref[i] = m * COEF + jnp.log2(full)
                delta = jnp.sum(
                    g_ref[i].astype(jnp.float32) * out.astype(jnp.float32), axis=1, keepdims=True
                )
                delta_ref[i] = lane_all(delta)
            else:
                m_ref[i] = m
                l_ref[i] = totals[u]
                acc_ref[i] = acc

        staggered((scores, weights, sums))
        return carry

    lax.fori_loop(0, NBLK // UNROLL, step, 0)


def forward_far(group, last, slots, bias, q, stats, kv, grad):
    entries = entries_of(group)
    extra = (grad,) if last else ()
    return pl.pallas_call(
        functools.partial(forward_far_kernel, group, last),
        out_shape=(HALF, STAT, STAT) if last else (STAT, STAT, STAT),
        in_specs=[SMEM, SMEM] + [VMEM] * (4 + len(kv) + len(extra)),
        out_specs=(VMEM,) * 3,
        scratch_shapes=forward_scratch(len(entries) * BLOCK),
        compiler_params=params(),
        cost_estimate=cost(16 * len(entries), 2, 1, 8 * MIB),
        name="forward_far",
    )(slots, bias, q, *stats, *kv, *extra)


def backward_scratch(rows, width, copies):
    return [
        pltpu.VMEM((rows, width), jnp.bfloat16),
        pltpu.VMEM((rows, width), jnp.bfloat16),
    ] * copies


CHUNK = 2
TIE = (4,)


def backward_far_kernel(group, first, *refs):
    count = len(group)
    slots, bias, q_ref, g_ref, lse_ref, delta_ref = refs[:6]
    kv = refs[6 : 6 + count]
    rest = refs[6 + count :]
    if not first:
        dqi_ref, rest = rest[0], rest[1:]
    dq_ref, part, acc = rest[0], rest[1 : 1 + count], rest[1 + count : 1 + 2 * count]
    scratch = rest[1 + 2 * count :]
    entries = entries_of(group)
    for a in acc:
        a[...] = jnp.zeros_like(a)

    def step(t, carry):
        def weights(u):
            i = t * UNROLL + u
            p_ref, ds_ref = scratch[2 * u : 2 * u + 2]
            q = q_ref[i]
            g = g_ref[i]
            lse = lse_ref[i]
            delta = delta_ref[i]
            offsets = [lse + bias_of(bias, entry) for entry in group]
            for e in range(0, len(entries), CHUNK):
                some = entries[e : e + CHUNK]
                s = nt(q, gather(kv, some, slots, i, 0))
                d = nt(g, gather(kv, some, slots, i, 1))
                for f, (n, c) in enumerate(some):
                    p = jnp.exp2(s[:, block(f)] * COEF - offsets[n])
                    p_ref[:, block(e + f)] = p.astype(jnp.bfloat16)
                    ds = p * (d[:, block(f)] - delta)
                    ds_ref[:, block(e + f)] = ds.astype(jnp.bfloat16)

        def sums(u):
            i = t * UNROLL + u
            p_ref, ds_ref = scratch[2 * u : 2 * u + 2]
            dq = nn(ds_ref[...], gather(kv, entries, slots, i, 0))
            dq_ref[i] = dq if first else dq + dqi_ref[i]
            dk = tn(ds_ref[...], q_ref[i])
            dv = tn(p_ref[...], g_ref[i])
            for e, (n, c) in enumerate(entries):
                acc[n][slots[i, c], 0] += dk[block(e)]
                acc[n][slots[i, c], 1] += dv[block(e)]

        staggered((weights, sums))
        return carry

    lax.fori_loop(0, NBLK // UNROLL, step, 0)
    for out, a in zip(part, acc):
        out[...] = a[...].astype(jnp.bfloat16)


def backward_far(group, slots, bias, q, g, lse, delta, kv, dq):
    entries = entries_of(group)
    extra = () if dq is None else (dq,)
    return pl.pallas_call(
        functools.partial(backward_far_kernel, group, dq is None),
        out_shape=(STAT,) + tuple(jax.ShapeDtypeStruct(x.shape, jnp.bfloat16) for x in kv),
        in_specs=[SMEM, SMEM] + [VMEM] * (4 + len(kv) + len(extra)),
        out_specs=(VMEM,) * (1 + len(kv)),
        scratch_shapes=[pltpu.VMEM(x.shape, jnp.float32) for x in kv]
        + backward_scratch(BLOCK, len(entries) * BLOCK, UNROLL),
        compiler_params=params(),
        cost_estimate=cost(16 * len(entries), 5, 1, 8 * MIB),
        name="backward_far",
    )(slots, bias, q, g, lse, delta, *kv, *extra)


LOCAL_ROWS = 2
LOCAL_COPIES = 4


def backward_local_kernel(
    q_ref, g_ref, lse_ref, delta_ref, k_ref, v_ref, dqi_ref, dq_ref, dk_ref, dv_ref, *scratch
):
    rows = LOCAL_ROWS * BLOCK
    width = NBLK * BLOCK
    dk_ref[...] = jnp.zeros_like(dk_ref)
    dv_ref[...] = jnp.zeros_like(dv_ref)

    def step(t, carry):
        def here(ref, u):
            first = (t * LOCAL_COPIES + u) * LOCAL_ROWS
            return ref[pl.ds(first, LOCAL_ROWS)].reshape(rows, 128)

        def weights(u):
            p_ref, ds_ref = scratch[2 * u : 2 * u + 2]
            q = here(q_ref, u)
            g = here(g_ref, u)
            lse = here(lse_ref, u)
            delta = here(delta_ref, u)
            for e in range(0, NBLK, CHUNK):
                s = nt(q, k_ref[e : e + CHUNK].reshape(CHUNK * BLOCK, HEAD))
                d = nt(g, v_ref[e : e + CHUNK].reshape(CHUNK * BLOCK, HEAD))
                for f in range(CHUNK):
                    p = jnp.exp2(s[:, block(f)] * COEF - lse)
                    p_ref[:, block(e + f)] = p.astype(jnp.bfloat16)
                    ds = p * (d[:, block(f)] - delta)
                    ds_ref[:, block(e + f)] = ds.astype(jnp.bfloat16)

        def sums(u):
            p_ref, ds_ref = scratch[2 * u : 2 * u + 2]
            dq = here(dqi_ref, u) + nn(ds_ref[...], k_ref[...].reshape(width, HEAD))
            first = (t * LOCAL_COPIES + u) * LOCAL_ROWS
            dq_ref[pl.ds(first, LOCAL_ROWS)] = (
                (dq * SCALE).astype(jnp.bfloat16).reshape(LOCAL_ROWS, BLOCK, HEAD)
            )
            dk_ref[...] += tn(ds_ref[...], here(q_ref, u)).reshape(NBLK, BLOCK, HEAD)
            dv_ref[...] += tn(p_ref[...], here(g_ref, u)).reshape(NBLK, BLOCK, HEAD)

        staggered((weights, sums), LOCAL_COPIES)
        return carry

    lax.fori_loop(0, NBLK // (LOCAL_ROWS * LOCAL_COPIES), step, 0)


def backward_local(q, g, lse, delta, k, v, dq):
    return pl.pallas_call(
        backward_local_kernel,
        out_shape=(HALF, STAT, STAT),
        in_specs=[VMEM] * 7,
        out_specs=(VMEM,) * 3,
        scratch_shapes=backward_scratch(LOCAL_ROWS * BLOCK, NBLK * BLOCK, LOCAL_COPIES),
        compiler_params=params(),
        cost_estimate=cost(256, 5, 1, 8 * MIB),
        name="backward_local",
    )(q, g, lse, delta, k, v, dq)


def finish_kernel(dk_ref, dv_ref, *refs):
    parts, (gk_ref, gv_ref) = refs[:-2], refs[-2:]
    for slot, own in enumerate(SLOT_BLOCK):
        dk = dk_ref[own]
        dv = dv_ref[own]
        for part in parts:
            if slot < part.shape[0]:
                dk += part[slot, 0].astype(jnp.float32)
                dv += part[slot, 1].astype(jnp.float32)
        gk_ref[own] = (dk * SCALE).astype(jnp.bfloat16)
        gv_ref[own] = dv.astype(jnp.bfloat16)


def finish(dk, dv, parts):
    return pl.pallas_call(
        finish_kernel,
        out_shape=(HALF, HALF),
        in_specs=[VMEM] * (2 + len(parts)),
        out_specs=(VMEM,) * 2,
        compiler_params=params(),
        name="finish",
    )(dk, dv, *parts)


def local(queries, keys, values, grad_out, block_lists):
    shape = (NBLK, BLOCK, HEAD)
    q, k, v, g = (x.reshape(shape) for x in (queries, keys, values, grad_out))
    position = lax.axis_index("seq")
    devices = lax.axis_size("seq")
    biases = [jnp.float32(0.0)] * 2
    for band, side, start, sel, by in PLAN:
        source = position - by
        valid = jnp.logical_and(source >= 0, source < devices)
        biases.append(jnp.where(valid, 0.0, BIG).astype(jnp.float32))
    bias = jnp.stack(biases)
    fetched = {}

    def fetch(sent, bands):
        for band, side, start, sel, by in PLAN:
            if band in bands:
                fetched[band, side] = shift(sent[band], by)

    def group(*bands):
        chosen = [e for e in PLAN if e[0] in bands]
        return chosen, [fetched[e[0], e[1]] for e in chosen]

    def hold(values, *bands):
        keys_of = [(e[0], e[1]) for e in group(*bands)[0]]
        values, got = lax.optimization_barrier((values, [fetched[x] for x in keys_of]))
        fetched.update(zip(keys_of, got))
        return values

    slots, everything, *few = pack(k, v, block_lists, NBLK, 4, 2)
    fetch(dict(zip((3, 4), few)), (3, 4))
    everything = hold(everything, *TIE)
    fetch({1: everything}, (1,))
    stats = forward_local(q, k, v)
    stats = hold(stats, 1)
    handed = hand_on(fetched[1, 0], fetched[1, 1])
    for side, by in ((0, 1), (1, -1)):
        fetched[2, side] = shift(handed[side], by)
    for bands, last in (((1, 3, 4), False), ((2,), True)):
        chosen, kv = group(*bands)
        stats = forward_far(chosen, last, slots, bias, q, stats, kv, g)
    out, lse, delta = stats

    def back(dq, *bands):
        chosen, kv = group(*bands)
        return backward_far(chosen, slots, bias, q, g, lse, delta, kv, dq)

    dq, *parts = back(None, 3, 4)
    returned = [shift(part, -e[4]) for part, e in zip(parts, group(3, 4)[0])]
    dq, *parts = back(dq, 2)
    parts, returned = lax.optimization_barrier((parts, returned))
    hop2 = [shift(part, -by) for part, by in zip(parts, (1, -1))]
    dq, *parts = back(dq, 1)
    parts = merge(parts, hop2)
    returned += [shift(part, -by) for part, by in zip(parts, (1, -1))]
    dq, dk, dv = backward_local(q, g, lse, delta, k, v, dq)
    gk, gv = finish(dk, dv, returned)
    flat = (NBLK * BLOCK, HEAD)
    return tuple(x.reshape(flat) for x in (out, dq, gk, gv))


def solution(mesh):
    spec = P(("dp", "seq"), None)
    return jax.shard_map(
        local,
        mesh=mesh,
        in_specs=(spec,) * 5,
        out_specs=(spec,) * 4,
        check_vma=False,
    )
```

```python
import functools
import math

import jax
import jax.numpy as jnp
from jax import lax
from jax.experimental import pallas as pl
from jax.experimental.pallas import tpu as pltpu
from jax.sharding import PartitionSpec as P

BLOCK = 128
HEAD = 128
NBLK = 16
FAR = 4
SCALE = 1.0 / math.sqrt(HEAD)
LOG2E = 1.4426950408889634
COEF = SCALE * LOG2E
BIG = 1e30
MIB = 2**20

SLOT_BLOCK = [0, 8, 4, 12, 2, 6, 10, 14, 1, 3, 5, 7, 9, 11, 13, 15]


def band_columns():
    plan = []
    start = 0
    for band in range(1, FAR + 1):
        stride = 2 ** (band - 1)
        sel = NBLK >> band
        for side, sign in enumerate((1, -1)):
            plan.append((band, side, start, sel, sign * stride))
            start += sel
    return plan


PLAN = band_columns()


def nt(a, b):
    return lax.dot_general(a, b, (((1,), (1,)), ((), ())), preferred_element_type=jnp.float32)


def nn(a, b):
    return lax.dot_general(a, b, (((1,), (0,)), ((), ())), preferred_element_type=jnp.float32)


def tn(a, b):
    return lax.dot_general(a, b, (((0,), (0,)), ((), ())), preferred_element_type=jnp.float32)


def shift(value, by):
    count = lax.axis_size("seq")
    first, last = max(0, -by), min(count, count - by)
    return lax.ppermute(value, "seq", [(s, s + by) for s in range(first, last)])


def params(limit=16):
    return pltpu.CompilerParams(vmem_limit_bytes=limit * MIB)


VMEM = pl.BlockSpec(memory_space=pltpu.VMEM)
SMEM = pl.BlockSpec(memory_space=pltpu.SMEM)


def cost(pairs, products, exps, moved):
    return pl.CostEstimate(
        flops=2 * pairs * products * BLOCK * BLOCK * HEAD,
        transcendentals=exps * pairs * BLOCK * BLOCK,
        bytes_accessed=moved,
    )


def slot_of(own):
    return jnp.where(
        (own & 1) == 1,
        8 + (own >> 1),
        jnp.where(
            (own & 3) == 2, 4 + (own >> 2), jnp.where((own & 7) == 4, 2 + (own >> 3), own >> 3)
        ),
    )


def pack_kernel(k_ref, v_ref, lists_ref, slots_ref, *outs):
    slots_ref[...] = slot_of(lists_ref[...])
    for slot, own in enumerate(SLOT_BLOCK):
        for out in outs:
            if slot < out.shape[0]:
                out[slot, 0] = k_ref[own]
                out[slot, 1] = v_ref[own]


def pack(key_blocks, value_blocks, lists, *sizes):
    return pl.pallas_call(
        pack_kernel,
        out_shape=(jax.ShapeDtypeStruct(lists.shape, jnp.int32),)
        + tuple(jax.ShapeDtypeStruct((n, 2, BLOCK, HEAD), jnp.bfloat16) for n in sizes),
        in_specs=[VMEM] * 3,
        out_specs=(VMEM,) * (1 + len(sizes)),
        compiler_params=params(),
        name="pack",
    )(key_blocks, value_blocks, lists)


def hand_on_kernel(*refs):
    count = len(refs) // 2
    for ref, out_ref in zip(refs[:count], refs[count:]):
        out_ref[...] = ref[: out_ref.shape[0]]


def hand_on(values):
    return pl.pallas_call(
        hand_on_kernel,
        out_shape=tuple(
            jax.ShapeDtypeStruct((x.shape[0] // 2,) + x.shape[1:], x.dtype) for x in values
        ),
        in_specs=[VMEM] * len(values),
        out_specs=(VMEM,) * len(values),
        compiler_params=params(),
        name="hand_on",
    )(*values)


def merge_kernel(*refs):
    count = len(refs) // 3
    for base, more, out in zip(refs[:count], refs[count : 2 * count], refs[2 * count :]):
        half = more.shape[0]
        total = base[:half].astype(jnp.float32) + more[...].astype(jnp.float32)
        out[:half] = total.astype(jnp.bfloat16)
        out[half:] = base[half:]


def merge(bases, mores):
    return pl.pallas_call(
        merge_kernel,
        out_shape=tuple(jax.ShapeDtypeStruct(x.shape, x.dtype) for x in bases),
        in_specs=[VMEM] * (2 * len(bases)),
        out_specs=(VMEM,) * len(bases),
        compiler_params=params(),
        name="merge",
    )(*bases, *mores)


def lane_all(x):
    return jnp.broadcast_to(x, (x.shape[0], 128))


def entries_of(group):
    return [
        (n, start + c) for n, (band, side, start, sel, by) in enumerate(group) for c in range(sel)
    ]


def gather(kv, entries, slots, i, which):
    return jnp.concatenate([kv[n][slots[i, c], which] for n, c in entries], axis=0)


def block(e):
    return slice(e * BLOCK, (e + 1) * BLOCK)


def bias_of(bias, entry):
    return bias[entry[0] * 2 + entry[1]]


STAT = jax.ShapeDtypeStruct((NBLK, BLOCK, 128), jnp.float32)
HALF = jax.ShapeDtypeStruct((NBLK, BLOCK, HEAD), jnp.bfloat16)
UNROLL = 4


def staggered(stages, copies=UNROLL):
    for tick in range(copies + len(stages) - 1):
        for n, stage in enumerate(stages):
            if 0 <= tick - n < copies:
                stage(tick - n)


def forward_local_kernel(q_ref, k_ref, v_ref, m_ref, l_ref, acc_ref, *scratch):
    width = NBLK * BLOCK

    def step(t, carry):
        def scores(u):
            scratch[2 * u][...] = nt(q_ref[t * UNROLL + u], k_ref[...].reshape(width, HEAD))

        def weights(u):
            s_ref, p_ref = scratch[2 * u : 2 * u + 2]
            top = s_ref[:, block(0)]
            for e in range(1, NBLK):
                top = jnp.maximum(top, s_ref[:, block(e)])
            m = lane_all(jnp.max(top, axis=1, keepdims=True))
            m_ref[t * UNROLL + u] = m
            total = jnp.zeros((BLOCK, 128), jnp.float32)
            for e in range(NBLK):
                p = jnp.exp2((s_ref[:, block(e)] - m) * COEF)
                total += p
                p_ref[:, block(e)] = p.astype(jnp.bfloat16)
            l_ref[t * UNROLL + u] = total

        def sums(u):
            acc_ref[t * UNROLL + u] = nn(scratch[2 * u + 1][...], v_ref[...].reshape(width, HEAD))

        staggered((scores, weights, sums))
        return carry

    lax.fori_loop(0, NBLK // UNROLL, step, 0)


def forward_scratch(width):
    return [
        pltpu.VMEM((BLOCK, width), jnp.float32),
        pltpu.VMEM((BLOCK, width), jnp.bfloat16),
    ] * UNROLL


def forward_local(q, k, v):
    return pl.pallas_call(
        forward_local_kernel,
        out_shape=(STAT, STAT, STAT),
        in_specs=[VMEM] * 3,
        out_specs=(VMEM,) * 3,
        scratch_shapes=forward_scratch(NBLK * BLOCK),
        compiler_params=params(),
        cost_estimate=cost(256, 2, 1, 5 * MIB),
        name="forward_local",
    )(q, k, v)


def forward_far_kernel(group, last, *refs):
    count = len(group)
    slots, bias, q_ref, mi_ref, li_ref, acci_ref = refs[:6]
    kv = refs[6 : 6 + count]
    rest = refs[6 + count :]
    if last:
        g_ref, out_ref, lse_ref, delta_ref = rest[:4]
        scratch = rest[4:]
    else:
        m_ref, l_ref, acc_ref = rest[:3]
        scratch = rest[3:]
    entries = entries_of(group)

    def step(t, carry):
        highs = [None] * UNROLL
        totals = [None] * UNROLL

        def scores(u):
            i = t * UNROLL + u
            scratch[2 * u][...] = nt(q_ref[i], gather(kv, entries, slots, i, 0))

        def weights(u):
            i = t * UNROLL + u
            s_ref, p_ref = scratch[2 * u : 2 * u + 2]
            top = None
            for n in range(count):
                own = [e for e in range(len(entries)) if entries[e][0] == n]
                part = s_ref[:, block(own[0])]
                for e in own[1:]:
                    part = jnp.maximum(part, s_ref[:, block(e)])
                part = part - bias_of(bias, group[n])
                top = part if top is None else jnp.maximum(top, part)
            m = jnp.maximum(mi_ref[i], lane_all(jnp.max(top, axis=1, keepdims=True)))
            total = li_ref[i] * jnp.exp2((mi_ref[i] - m) * COEF)
            offsets = [m + bias_of(bias, entry) for entry in group]
            for e, (n, c) in enumerate(entries):
                p = jnp.exp2((s_ref[:, block(e)] - offsets[n]) * COEF)
                total += p
                p_ref[:, block(e)] = p.astype(jnp.bfloat16)
            highs[u] = m
            totals[u] = total

        def sums(u):
            i = t * UNROLL + u
            m = highs[u]
            acc = acci_ref[i] * jnp.exp2((mi_ref[i] - m) * COEF)
            acc += nn(scratch[2 * u + 1][...], gather(kv, entries, slots, i, 1))
            if last:
                full = lane_all(jnp.sum(totals[u], axis=1, keepdims=True))
                out = (acc / full).astype(jnp.bfloat16)
                out_ref[i] = out
                lse_ref[i] = m * COEF + jnp.log2(full)
                delta = jnp.sum(
                    g_ref[i].astype(jnp.float32) * out.astype(jnp.float32), axis=1, keepdims=True
                )
                delta_ref[i] = lane_all(delta)
            else:
                m_ref[i] = m
                l_ref[i] = totals[u]
                acc_ref[i] = acc

        staggered((scores, weights, sums))
        return carry

    lax.fori_loop(0, NBLK // UNROLL, step, 0)


def forward_far(group, last, slots, bias, q, stats, kv, grad):
    entries = entries_of(group)
    extra = (grad,) if last else ()
    return pl.pallas_call(
        functools.partial(forward_far_kernel, group, last),
        out_shape=(HALF, STAT, STAT) if last else (STAT, STAT, STAT),
        in_specs=[SMEM, SMEM] + [VMEM] * (4 + len(kv) + len(extra)),
        out_specs=(VMEM,) * 3,
        scratch_shapes=forward_scratch(len(entries) * BLOCK),
        compiler_params=params(),
        cost_estimate=cost(16 * len(entries), 2, 1, 8 * MIB),
        name="forward_far",
    )(slots, bias, q, *stats, *kv, *extra)


def backward_scratch(rows, width, copies):
    return [
        pltpu.VMEM((rows, width), jnp.bfloat16),
        pltpu.VMEM((rows, width), jnp.bfloat16),
    ] * copies


CHUNK = 2


def backward_far_kernel(group, first, *refs):
    count = len(group)
    slots, bias, q_ref, g_ref, lse_ref, delta_ref = refs[:6]
    kv = refs[6 : 6 + count]
    rest = refs[6 + count :]
    if not first:
        dqi_ref, rest = rest[0], rest[1:]
    dq_ref, part, acc = rest[0], rest[1 : 1 + count], rest[1 + count : 1 + 2 * count]
    scratch = rest[1 + 2 * count :]
    entries = entries_of(group)
    for a in acc:
        a[...] = jnp.zeros_like(a)

    def step(t, carry):
        def weights(u):
            i = t * UNROLL + u
            p_ref, ds_ref = scratch[2 * u : 2 * u + 2]
            q = q_ref[i]
            g = g_ref[i]
            lse = lse_ref[i]
            delta = delta_ref[i]
            offsets = [lse + bias_of(bias, entry) for entry in group]
            for e in range(0, len(entries), CHUNK):
                some = entries[e : e + CHUNK]
                s = nt(q, gather(kv, some, slots, i, 0))
                d = nt(g, gather(kv, some, slots, i, 1))
                for f, (n, c) in enumerate(some):
                    p = jnp.exp2(s[:, block(f)] * COEF - offsets[n])
                    p_ref[:, block(e + f)] = p.astype(jnp.bfloat16)
                    ds = p * (d[:, block(f)] - delta)
                    ds_ref[:, block(e + f)] = ds.astype(jnp.bfloat16)

        def sums(u):
            i = t * UNROLL + u
            p_ref, ds_ref = scratch[2 * u : 2 * u + 2]
            dq = nn(ds_ref[...], gather(kv, entries, slots, i, 0))
            dq_ref[i] = dq if first else dq + dqi_ref[i]
            dk = tn(ds_ref[...], q_ref[i])
            dv = tn(p_ref[...], g_ref[i])
            for e, (n, c) in enumerate(entries):
                acc[n][slots[i, c], 0] += dk[block(e)]
                acc[n][slots[i, c], 1] += dv[block(e)]

        staggered((weights, sums))
        return carry

    lax.fori_loop(0, NBLK // UNROLL, step, 0)
    for out, a in zip(part, acc):
        out[...] = a[...].astype(jnp.bfloat16)


def backward_far(group, slots, bias, q, g, lse, delta, kv, dq):
    entries = entries_of(group)
    extra = () if dq is None else (dq,)
    return pl.pallas_call(
        functools.partial(backward_far_kernel, group, dq is None),
        out_shape=(STAT,) + tuple(jax.ShapeDtypeStruct(x.shape, jnp.bfloat16) for x in kv),
        in_specs=[SMEM, SMEM] + [VMEM] * (4 + len(kv) + len(extra)),
        out_specs=(VMEM,) * (1 + len(kv)),
        scratch_shapes=[pltpu.VMEM(x.shape, jnp.float32) for x in kv]
        + backward_scratch(BLOCK, len(entries) * BLOCK, UNROLL),
        compiler_params=params(),
        cost_estimate=cost(16 * len(entries), 5, 1, 8 * MIB),
        name="backward_far",
    )(slots, bias, q, g, lse, delta, *kv, *extra)


LOCAL_ROWS = 2
LOCAL_COPIES = 4


def backward_local_kernel(
    q_ref, g_ref, lse_ref, delta_ref, k_ref, v_ref, dqi_ref, dq_ref, dk_ref, dv_ref, *scratch
):
    rows = LOCAL_ROWS * BLOCK
    width = NBLK * BLOCK
    dk_ref[...] = jnp.zeros_like(dk_ref)
    dv_ref[...] = jnp.zeros_like(dv_ref)

    def step(t, carry):
        def here(ref, u):
            first = (t * LOCAL_COPIES + u) * LOCAL_ROWS
            return ref[pl.ds(first, LOCAL_ROWS)].reshape(rows, 128)

        def weights(u):
            p_ref, ds_ref = scratch[2 * u : 2 * u + 2]
            q = here(q_ref, u)
            g = here(g_ref, u)
            lse = here(lse_ref, u)
            delta = here(delta_ref, u)
            for e in range(0, NBLK, CHUNK):
                s = nt(q, k_ref[e : e + CHUNK].reshape(CHUNK * BLOCK, HEAD))
                d = nt(g, v_ref[e : e + CHUNK].reshape(CHUNK * BLOCK, HEAD))
                for f in range(CHUNK):
                    p = jnp.exp2(s[:, block(f)] * COEF - lse)
                    p_ref[:, block(e + f)] = p.astype(jnp.bfloat16)
                    ds = p * (d[:, block(f)] - delta)
                    ds_ref[:, block(e + f)] = ds.astype(jnp.bfloat16)

        def sums(u):
            p_ref, ds_ref = scratch[2 * u : 2 * u + 2]
            dq = here(dqi_ref, u) + nn(ds_ref[...], k_ref[...].reshape(width, HEAD))
            first = (t * LOCAL_COPIES + u) * LOCAL_ROWS
            dq_ref[pl.ds(first, LOCAL_ROWS)] = (
                (dq * SCALE).astype(jnp.bfloat16).reshape(LOCAL_ROWS, BLOCK, HEAD)
            )
            dk_ref[...] += tn(ds_ref[...], here(q_ref, u)).reshape(NBLK, BLOCK, HEAD)
            dv_ref[...] += tn(p_ref[...], here(g_ref, u)).reshape(NBLK, BLOCK, HEAD)

        staggered((weights, sums), LOCAL_COPIES)
        return carry

    lax.fori_loop(0, NBLK // (LOCAL_ROWS * LOCAL_COPIES), step, 0)


def backward_local(q, g, lse, delta, k, v, dq):
    return pl.pallas_call(
        backward_local_kernel,
        out_shape=(HALF, STAT, STAT),
        in_specs=[VMEM] * 7,
        out_specs=(VMEM,) * 3,
        scratch_shapes=backward_scratch(LOCAL_ROWS * BLOCK, NBLK * BLOCK, LOCAL_COPIES),
        compiler_params=params(),
        cost_estimate=cost(256, 5, 1, 8 * MIB),
        name="backward_local",
    )(q, g, lse, delta, k, v, dq)


def finish_kernel(dk_ref, dv_ref, *refs):
    parts, (gk_ref, gv_ref) = refs[:-2], refs[-2:]
    for slot, own in enumerate(SLOT_BLOCK):
        dk = dk_ref[own]
        dv = dv_ref[own]
        for part in parts:
            if slot < part.shape[0]:
                dk += part[slot, 0].astype(jnp.float32)
                dv += part[slot, 1].astype(jnp.float32)
        gk_ref[own] = (dk * SCALE).astype(jnp.bfloat16)
        gv_ref[own] = dv.astype(jnp.bfloat16)


def finish(dk, dv, parts):
    return pl.pallas_call(
        finish_kernel,
        out_shape=(HALF, HALF),
        in_specs=[VMEM] * (2 + len(parts)),
        out_specs=(VMEM,) * 2,
        compiler_params=params(),
        name="finish",
    )(dk, dv, *parts)


def local(queries, keys, values, grad_out, block_lists):
    shape = (NBLK, BLOCK, HEAD)
    q, k, v, g = (x.reshape(shape) for x in (queries, keys, values, grad_out))
    position = lax.axis_index("seq")
    devices = lax.axis_size("seq")
    biases = [jnp.float32(0.0)] * 2
    for band, side, start, sel, by in PLAN:
        source = position - by
        valid = jnp.logical_and(source >= 0, source < devices)
        biases.append(jnp.where(valid, 0.0, BIG).astype(jnp.float32))
    bias = jnp.stack(biases)
    fetched = {}

    def fetch(sent, bands):
        for band, side, start, sel, by in PLAN:
            if band in bands:
                fetched[band, side] = shift(sent[band], by)

    def group(*bands):
        chosen = [e for e in PLAN if e[0] in bands]
        return chosen, [fetched[e[0], e[1]] for e in chosen]

    def hold(values, *bands):
        keys_of = [(e[0], e[1]) for e in group(*bands)[0]]
        values, got = lax.optimization_barrier((values, [fetched[x] for x in keys_of]))
        fetched.update(zip(keys_of, got))
        return values

    slots, near, next_near, far = pack(k, v, block_lists, NBLK, 4, 2)
    fetch({1: near, 4: far}, (1, 4))
    stats = forward_local(q, k, v)
    stats, next_near = hold((stats, next_near), 1)
    hops = ((1, 0, 1), (1, 1, -1), (3, 0, 4), (3, 1, -4))
    handed = hand_on([fetched[1, 0], fetched[1, 1]])
    for (band, side, by), part in zip(hops, handed):
        fetched[band + 1, side] = shift(part, by)
    fetch({3: next_near}, (3,))
    for bands, last in (((1,), False), ((2, 3, 4), True)):
        chosen, kv = group(*bands)
        stats = forward_far(chosen, last, slots, bias, q, stats, kv, g)
    out, lse, delta = stats

    def back(dq, *bands):
        chosen, kv = group(*bands)
        return backward_far(chosen, slots, bias, q, g, lse, delta, kv, dq)

    dq, *parts = back(None, 2, 4)
    hop = [shift(part, -by) for part, (band, side, by) in zip(parts, hops)]
    dq, *parts = back(dq, 1, 3)
    parts = merge(parts, hop)
    returned = [shift(part, -by) for part, (band, side, by) in zip(parts, hops)]
    dq, dk, dv = backward_local(q, g, lse, delta, k, v, dq)
    gk, gv = finish(dk, dv, returned)
    flat = (NBLK * BLOCK, HEAD)
    return tuple(x.reshape(flat) for x in (out, dq, gk, gv))


def solution(mesh):
    spec = P(("dp", "seq"), None)
    return jax.shard_map(
        local,
        mesh=mesh,
        in_specs=(spec,) * 5,
        out_specs=(spec,) * 4,
        check_vma=False,
    )
```

```python
import functools
import math

import jax
import jax.numpy as jnp
from jax import lax
from jax.experimental import pallas as pl
from jax.experimental.pallas import tpu as pltpu
from jax.sharding import PartitionSpec as P

BLOCK = 128
HEAD = 128
NBLK = 16
FAR = 4
SCALE = 1.0 / math.sqrt(HEAD)
LOG2E = 1.4426950408889634
COEF = SCALE * LOG2E
BIG = 1e30
MIB = 2**20

SLOT_BLOCK = [0, 8, 4, 12, 2, 6, 10, 14, 1, 3, 5, 7, 9, 11, 13, 15]


def band_columns():
    plan = []
    start = 0
    for band in range(1, FAR + 1):
        stride = 2 ** (band - 1)
        sel = NBLK >> band
        for side, sign in enumerate((1, -1)):
            plan.append((band, side, start, sel, sign * stride))
            start += sel
    return plan


PLAN = band_columns()


def nt(a, b):
    return lax.dot_general(a, b, (((1,), (1,)), ((), ())), preferred_element_type=jnp.float32)


def nn(a, b):
    return lax.dot_general(a, b, (((1,), (0,)), ((), ())), preferred_element_type=jnp.float32)


def tn(a, b):
    return lax.dot_general(a, b, (((0,), (0,)), ((), ())), preferred_element_type=jnp.float32)


def shift(value, by):
    count = lax.axis_size("seq")
    first, last = max(0, -by), min(count, count - by)
    return lax.ppermute(value, "seq", [(s, s + by) for s in range(first, last)])


def params(limit=16):
    return pltpu.CompilerParams(vmem_limit_bytes=limit * MIB)


VMEM = pl.BlockSpec(memory_space=pltpu.VMEM)
SMEM = pl.BlockSpec(memory_space=pltpu.SMEM)


def cost(pairs, products, exps, moved):
    return pl.CostEstimate(
        flops=2 * pairs * products * BLOCK * BLOCK * HEAD,
        transcendentals=exps * pairs * BLOCK * BLOCK,
        bytes_accessed=moved,
    )


def slot_of(own):
    return jnp.where(
        (own & 1) == 1,
        8 + (own >> 1),
        jnp.where(
            (own & 3) == 2, 4 + (own >> 2), jnp.where((own & 7) == 4, 2 + (own >> 3), own >> 3)
        ),
    )


def pack_kernel(k_ref, v_ref, lists_ref, slots_ref, *outs):
    slots_ref[...] = slot_of(lists_ref[...])
    for slot, own in enumerate(SLOT_BLOCK):
        for out in outs:
            if slot < out.shape[0]:
                out[slot, 0] = k_ref[own]
                out[slot, 1] = v_ref[own]


def pack(key_blocks, value_blocks, lists, *sizes):
    return pl.pallas_call(
        pack_kernel,
        out_shape=(jax.ShapeDtypeStruct(lists.shape, jnp.int32),)
        + tuple(jax.ShapeDtypeStruct((n, 2, BLOCK, HEAD), jnp.bfloat16) for n in sizes),
        in_specs=[VMEM] * 3,
        out_specs=(VMEM,) * (1 + len(sizes)),
        compiler_params=params(),
        name="pack",
    )(key_blocks, value_blocks, lists)


def hand_on_kernel(*refs):
    count = len(refs) // 2
    for ref, out_ref in zip(refs[:count], refs[count:]):
        out_ref[...] = ref[: out_ref.shape[0]]


def hand_on(values):
    return pl.pallas_call(
        hand_on_kernel,
        out_shape=tuple(
            jax.ShapeDtypeStruct((x.shape[0] // 2,) + x.shape[1:], x.dtype) for x in values
        ),
        in_specs=[VMEM] * len(values),
        out_specs=(VMEM,) * len(values),
        compiler_params=params(),
        name="hand_on",
    )(*values)


def merge_kernel(*refs):
    count = len(refs) // 3
    for base, more, out in zip(refs[:count], refs[count : 2 * count], refs[2 * count :]):
        half = more.shape[0]
        total = base[:half].astype(jnp.float32) + more[...].astype(jnp.float32)
        out[:half] = total.astype(jnp.bfloat16)
        out[half:] = base[half:]


def merge(bases, mores):
    return pl.pallas_call(
        merge_kernel,
        out_shape=tuple(jax.ShapeDtypeStruct(x.shape, x.dtype) for x in bases),
        in_specs=[VMEM] * (2 * len(bases)),
        out_specs=(VMEM,) * len(bases),
        compiler_params=params(),
        name="merge",
    )(*bases, *mores)


def lane_all(x):
    return jnp.broadcast_to(x, (x.shape[0], 128))


def entries_of(group):
    return [
        (n, start + c) for n, (band, side, start, sel, by) in enumerate(group) for c in range(sel)
    ]


def gather(kv, entries, slots, i, which):
    return jnp.concatenate([kv[n][slots[i, c], which] for n, c in entries], axis=0)


def block(e):
    return slice(e * BLOCK, (e + 1) * BLOCK)


def bias_of(bias, entry):
    return bias[entry[0] * 2 + entry[1]]


STAT = jax.ShapeDtypeStruct((NBLK, BLOCK, 128), jnp.float32)
HALF = jax.ShapeDtypeStruct((NBLK, BLOCK, HEAD), jnp.bfloat16)
UNROLL = 4


def staggered(stages, copies=UNROLL):
    for tick in range(copies + len(stages) - 1):
        for n, stage in enumerate(stages):
            if 0 <= tick - n < copies:
                stage(tick - n)


def forward_local_kernel(q_ref, k_ref, v_ref, m_ref, l_ref, acc_ref, *scratch):
    width = NBLK * BLOCK

    def step(t, carry):
        def scores(u):
            scratch[2 * u][...] = nt(q_ref[t * UNROLL + u], k_ref[...].reshape(width, HEAD))

        def weights(u):
            s_ref, p_ref = scratch[2 * u : 2 * u + 2]
            top = s_ref[:, block(0)]
            for e in range(1, NBLK):
                top = jnp.maximum(top, s_ref[:, block(e)])
            m = lane_all(jnp.max(top, axis=1, keepdims=True))
            m_ref[t * UNROLL + u] = m
            total = jnp.zeros((BLOCK, 128), jnp.float32)
            for e in range(NBLK):
                p = jnp.exp2((s_ref[:, block(e)] - m) * COEF)
                total += p
                p_ref[:, block(e)] = p.astype(jnp.bfloat16)
            l_ref[t * UNROLL + u] = total

        def sums(u):
            acc_ref[t * UNROLL + u] = nn(scratch[2 * u + 1][...], v_ref[...].reshape(width, HEAD))

        staggered((scores, weights, sums))
        return carry

    lax.fori_loop(0, NBLK // UNROLL, step, 0)


def forward_scratch(width):
    return [
        pltpu.VMEM((BLOCK, width), jnp.float32),
        pltpu.VMEM((BLOCK, width), jnp.bfloat16),
    ] * UNROLL


def forward_local(q, k, v):
    return pl.pallas_call(
        forward_local_kernel,
        out_shape=(STAT, STAT, STAT),
        in_specs=[VMEM] * 3,
        out_specs=(VMEM,) * 3,
        scratch_shapes=forward_scratch(NBLK * BLOCK),
        compiler_params=params(),
        cost_estimate=cost(256, 2, 1, 5 * MIB),
        name="forward_local",
    )(q, k, v)


def forward_far_kernel(group, last, *refs):
    count = len(group)
    slots, bias, q_ref, mi_ref, li_ref, acci_ref = refs[:6]
    kv = refs[6 : 6 + count]
    rest = refs[6 + count :]
    if last:
        g_ref, out_ref, lse_ref, delta_ref = rest[:4]
        scratch = rest[4:]
    else:
        m_ref, l_ref, acc_ref = rest[:3]
        scratch = rest[3:]
    entries = entries_of(group)

    def step(t, carry):
        highs = [None] * UNROLL
        totals = [None] * UNROLL

        def scores(u):
            i = t * UNROLL + u
            scratch[2 * u][...] = nt(q_ref[i], gather(kv, entries, slots, i, 0))

        def weights(u):
            i = t * UNROLL + u
            s_ref, p_ref = scratch[2 * u : 2 * u + 2]
            top = None
            for n in range(count):
                own = [e for e in range(len(entries)) if entries[e][0] == n]
                part = s_ref[:, block(own[0])]
                for e in own[1:]:
                    part = jnp.maximum(part, s_ref[:, block(e)])
                part = part - bias_of(bias, group[n])
                top = part if top is None else jnp.maximum(top, part)
            m = jnp.maximum(mi_ref[i], lane_all(jnp.max(top, axis=1, keepdims=True)))
            total = li_ref[i] * jnp.exp2((mi_ref[i] - m) * COEF)
            offsets = [m + bias_of(bias, entry) for entry in group]
            for e, (n, c) in enumerate(entries):
                p = jnp.exp2((s_ref[:, block(e)] - offsets[n]) * COEF)
                total += p
                p_ref[:, block(e)] = p.astype(jnp.bfloat16)
            highs[u] = m
            totals[u] = total

        def sums(u):
            i = t * UNROLL + u
            m = highs[u]
            acc = acci_ref[i] * jnp.exp2((mi_ref[i] - m) * COEF)
            acc += nn(scratch[2 * u + 1][...], gather(kv, entries, slots, i, 1))
            if last:
                full = lane_all(jnp.sum(totals[u], axis=1, keepdims=True))
                out = (acc / full).astype(jnp.bfloat16)
                out_ref[i] = out
                lse_ref[i] = m * COEF + jnp.log2(full)
                delta = jnp.sum(
                    g_ref[i].astype(jnp.float32) * out.astype(jnp.float32), axis=1, keepdims=True
                )
                delta_ref[i] = lane_all(delta)
            else:
                m_ref[i] = m
                l_ref[i] = totals[u]
                acc_ref[i] = acc

        staggered((scores, weights, sums))
        return carry

    lax.fori_loop(0, NBLK // UNROLL, step, 0)


def forward_far(group, last, slots, bias, q, stats, kv, grad):
    entries = entries_of(group)
    extra = (grad,) if last else ()
    return pl.pallas_call(
        functools.partial(forward_far_kernel, group, last),
        out_shape=(HALF, STAT, STAT) if last else (STAT, STAT, STAT),
        in_specs=[SMEM, SMEM] + [VMEM] * (4 + len(kv) + len(extra)),
        out_specs=(VMEM,) * 3,
        scratch_shapes=forward_scratch(len(entries) * BLOCK),
        compiler_params=params(),
        cost_estimate=cost(16 * len(entries), 2, 1, 8 * MIB),
        name="forward_far",
    )(slots, bias, q, *stats, *kv, *extra)


def backward_scratch(rows, width, copies):
    return [
        pltpu.VMEM((rows, width), jnp.bfloat16),
        pltpu.VMEM((rows, width), jnp.bfloat16),
    ] * copies


CHUNK = 2


def backward_far_kernel(group, first, *refs):
    count = len(group)
    slots, bias, q_ref, g_ref, lse_ref, delta_ref = refs[:6]
    kv = refs[6 : 6 + count]
    rest = refs[6 + count :]
    if not first:
        dqi_ref, rest = rest[0], rest[1:]
    dq_ref, part, acc = rest[0], rest[1 : 1 + count], rest[1 + count : 1 + 2 * count]
    scratch = rest[1 + 2 * count :]
    entries = entries_of(group)
    for a in acc:
        a[...] = jnp.zeros_like(a)

    def step(t, carry):
        def weights(u):
            i = t * UNROLL + u
            p_ref, ds_ref = scratch[2 * u : 2 * u + 2]
            q = q_ref[i]
            g = g_ref[i]
            lse = lse_ref[i]
            delta = delta_ref[i]
            offsets = [lse + bias_of(bias, entry) for entry in group]
            for e in range(0, len(entries), CHUNK):
                some = entries[e : e + CHUNK]
                s = nt(q, gather(kv, some, slots, i, 0))
                d = nt(g, gather(kv, some, slots, i, 1))
                for f, (n, c) in enumerate(some):
                    p = jnp.exp2(s[:, block(f)] * COEF - offsets[n])
                    p_ref[:, block(e + f)] = p.astype(jnp.bfloat16)
                    ds = p * (d[:, block(f)] - delta)
                    ds_ref[:, block(e + f)] = ds.astype(jnp.bfloat16)

        def sums(u):
            i = t * UNROLL + u
            p_ref, ds_ref = scratch[2 * u : 2 * u + 2]
            dq = nn(ds_ref[...], gather(kv, entries, slots, i, 0))
            dq_ref[i] = dq if first else dq + dqi_ref[i]
            dk = tn(ds_ref[...], q_ref[i])
            dv = tn(p_ref[...], g_ref[i])
            for e, (n, c) in enumerate(entries):
                acc[n][slots[i, c], 0] += dk[block(e)]
                acc[n][slots[i, c], 1] += dv[block(e)]

        staggered((weights, sums))
        return carry

    lax.fori_loop(0, NBLK // UNROLL, step, 0)
    for out, a in zip(part, acc):
        out[...] = a[...].astype(jnp.bfloat16)


def backward_far(group, slots, bias, q, g, lse, delta, kv, dq):
    entries = entries_of(group)
    extra = () if dq is None else (dq,)
    return pl.pallas_call(
        functools.partial(backward_far_kernel, group, dq is None),
        out_shape=(STAT,) + tuple(jax.ShapeDtypeStruct(x.shape, jnp.bfloat16) for x in kv),
        in_specs=[SMEM, SMEM] + [VMEM] * (4 + len(kv) + len(extra)),
        out_specs=(VMEM,) * (1 + len(kv)),
        scratch_shapes=[pltpu.VMEM(x.shape, jnp.float32) for x in kv]
        + backward_scratch(BLOCK, len(entries) * BLOCK, UNROLL),
        compiler_params=params(),
        cost_estimate=cost(16 * len(entries), 5, 1, 8 * MIB),
        name="backward_far",
    )(slots, bias, q, g, lse, delta, *kv, *extra)


LOCAL_ROWS = 2
LOCAL_COPIES = 4


def backward_local_kernel(
    q_ref, g_ref, lse_ref, delta_ref, k_ref, v_ref, dqi_ref, dq_ref, dk_ref, dv_ref, *scratch
):
    rows = LOCAL_ROWS * BLOCK
    width = NBLK * BLOCK
    dk_ref[...] = jnp.zeros_like(dk_ref)
    dv_ref[...] = jnp.zeros_like(dv_ref)

    def step(t, carry):
        def here(ref, u):
            first = (t * LOCAL_COPIES + u) * LOCAL_ROWS
            return ref[pl.ds(first, LOCAL_ROWS)].reshape(rows, 128)

        def weights(u):
            p_ref, ds_ref = scratch[2 * u : 2 * u + 2]
            q = here(q_ref, u)
            g = here(g_ref, u)
            lse = here(lse_ref, u)
            delta = here(delta_ref, u)
            for e in range(0, NBLK, CHUNK):
                s = nt(q, k_ref[e : e + CHUNK].reshape(CHUNK * BLOCK, HEAD))
                d = nt(g, v_ref[e : e + CHUNK].reshape(CHUNK * BLOCK, HEAD))
                for f in range(CHUNK):
                    p = jnp.exp2(s[:, block(f)] * COEF - lse)
                    p_ref[:, block(e + f)] = p.astype(jnp.bfloat16)
                    ds = p * (d[:, block(f)] - delta)
                    ds_ref[:, block(e + f)] = ds.astype(jnp.bfloat16)

        def sums(u):
            p_ref, ds_ref = scratch[2 * u : 2 * u + 2]
            dq = here(dqi_ref, u) + nn(ds_ref[...], k_ref[...].reshape(width, HEAD))
            first = (t * LOCAL_COPIES + u) * LOCAL_ROWS
            dq_ref[pl.ds(first, LOCAL_ROWS)] = (
                (dq * SCALE).astype(jnp.bfloat16).reshape(LOCAL_ROWS, BLOCK, HEAD)
            )
            dk_ref[...] += tn(ds_ref[...], here(q_ref, u)).reshape(NBLK, BLOCK, HEAD)
            dv_ref[...] += tn(p_ref[...], here(g_ref, u)).reshape(NBLK, BLOCK, HEAD)

        staggered((weights, sums), LOCAL_COPIES)
        return carry

    lax.fori_loop(0, NBLK // (LOCAL_ROWS * LOCAL_COPIES), step, 0)


def backward_local(q, g, lse, delta, k, v, dq):
    return pl.pallas_call(
        backward_local_kernel,
        out_shape=(HALF, STAT, STAT),
        in_specs=[VMEM] * 7,
        out_specs=(VMEM,) * 3,
        scratch_shapes=backward_scratch(LOCAL_ROWS * BLOCK, NBLK * BLOCK, LOCAL_COPIES),
        compiler_params=params(),
        cost_estimate=cost(256, 5, 1, 8 * MIB),
        name="backward_local",
    )(q, g, lse, delta, k, v, dq)


def finish_kernel(dk_ref, dv_ref, *refs):
    parts, (gk_ref, gv_ref) = refs[:-2], refs[-2:]
    for slot, own in enumerate(SLOT_BLOCK):
        dk = dk_ref[own]
        dv = dv_ref[own]
        for part in parts:
            if slot < part.shape[0]:
                dk += part[slot, 0].astype(jnp.float32)
                dv += part[slot, 1].astype(jnp.float32)
        gk_ref[own] = (dk * SCALE).astype(jnp.bfloat16)
        gv_ref[own] = dv.astype(jnp.bfloat16)


def finish(dk, dv, parts):
    return pl.pallas_call(
        finish_kernel,
        out_shape=(HALF, HALF),
        in_specs=[VMEM] * (2 + len(parts)),
        out_specs=(VMEM,) * 2,
        compiler_params=params(),
        name="finish",
    )(dk, dv, *parts)


def local(queries, keys, values, grad_out, block_lists):
    shape = (NBLK, BLOCK, HEAD)
    q, k, v, g = (x.reshape(shape) for x in (queries, keys, values, grad_out))
    position = lax.axis_index("seq")
    devices = lax.axis_size("seq")
    biases = [jnp.float32(0.0)] * 2
    for band, side, start, sel, by in PLAN:
        source = position - by
        valid = jnp.logical_and(source >= 0, source < devices)
        biases.append(jnp.where(valid, 0.0, BIG).astype(jnp.float32))
    bias = jnp.stack(biases)
    fetched = {}

    def fetch(sent, bands):
        for band, side, start, sel, by in PLAN:
            if band in bands:
                fetched[band, side] = shift(sent[band], by)

    def group(*bands):
        chosen = [e for e in PLAN if e[0] in bands]
        return chosen, [fetched[e[0], e[1]] for e in chosen]

    def hold(values, *bands):
        keys_of = [(e[0], e[1]) for e in group(*bands)[0]]
        values, got = lax.optimization_barrier((values, [fetched[x] for x in keys_of]))
        fetched.update(zip(keys_of, got))
        return values

    slots, near, next_near, far = pack(k, v, block_lists, NBLK, 4, 2)
    fetch({1: near, 4: far}, (1, 4))
    stats = forward_local(q, k, v)
    stats, next_near = hold((stats, next_near), 1)
    hops = ((1, 0, 1), (1, 1, -1), (3, 0, 4), (3, 1, -4))
    handed = hand_on([fetched[1, 0], fetched[1, 1]])
    for (band, side, by), part in zip(hops, handed):
        fetched[band + 1, side] = shift(part, by)
    fetch({3: next_near}, (3,))
    for bands, last in (((1,), False), ((2, 3, 4), True)):
        chosen, kv = group(*bands)
        stats = forward_far(chosen, last, slots, bias, q, stats, kv, g)
    out, lse, delta = stats

    def back(dq, *bands):
        chosen, kv = group(*bands)
        return backward_far(chosen, slots, bias, q, g, lse, delta, kv, dq)

    dq, *parts = back(None, 2, 4)
    hop = [shift(part, -by) for part, (band, side, by) in zip(parts, hops)]
    returned = []
    for n, band in ((0, 1), (2, 3)):
        dq, *parts = back(dq, band)
        parts, hop = lax.optimization_barrier((parts, hop))
        parts = merge(parts, hop[n : n + 2])
        returned += [
            shift(part, -by) for part, (own, side, by) in zip(parts, hops[n : n + 2])
        ]
    dq, dk, dv = backward_local(q, g, lse, delta, k, v, dq)
    gk, gv = finish(dk, dv, returned)
    flat = (NBLK * BLOCK, HEAD)
    return tuple(x.reshape(flat) for x in (out, dq, gk, gv))


def solution(mesh):
    spec = P(("dp", "seq"), None)
    return jax.shard_map(
        local,
        mesh=mesh,
        in_specs=(spec,) * 5,
        out_specs=(spec,) * 4,
        check_vma=False,
    )
```

```python
import functools
import math

import jax
import jax.numpy as jnp
from jax import lax
from jax.experimental import pallas as pl
from jax.experimental.pallas import tpu as pltpu
from jax.sharding import PartitionSpec as P

BLOCK = 128
HEAD = 128
NBLK = 16
FAR = 4
SCALE = 1.0 / math.sqrt(HEAD)
LOG2E = 1.4426950408889634
COEF = SCALE * LOG2E
BIG = 1e30
MIB = 2**20

SLOT_BLOCK = [0, 8, 4, 12, 2, 6, 10, 14, 1, 3, 5, 7, 9, 11, 13, 15]


def band_columns():
    plan = []
    start = 0
    for band in range(1, FAR + 1):
        stride = 2 ** (band - 1)
        sel = NBLK >> band
        for side, sign in enumerate((1, -1)):
            plan.append((band, side, start, sel, sign * stride))
            start += sel
    return plan


PLAN = band_columns()


def nt(a, b):
    return lax.dot_general(a, b, (((1,), (1,)), ((), ())), preferred_element_type=jnp.float32)


def nn(a, b):
    return lax.dot_general(a, b, (((1,), (0,)), ((), ())), preferred_element_type=jnp.float32)


def tn(a, b):
    return lax.dot_general(a, b, (((0,), (0,)), ((), ())), preferred_element_type=jnp.float32)


def shift(value, by):
    count = lax.axis_size("seq")
    first, last = max(0, -by), min(count, count - by)
    return lax.ppermute(value, "seq", [(s, s + by) for s in range(first, last)])


def params(limit=16):
    return pltpu.CompilerParams(vmem_limit_bytes=limit * MIB)


VMEM = pl.BlockSpec(memory_space=pltpu.VMEM)
SMEM = pl.BlockSpec(memory_space=pltpu.SMEM)


def cost(pairs, products, exps, moved):
    return pl.CostEstimate(
        flops=2 * pairs * products * BLOCK * BLOCK * HEAD,
        transcendentals=exps * pairs * BLOCK * BLOCK,
        bytes_accessed=moved,
    )


def slot_of(own):
    return jnp.where(
        (own & 1) == 1,
        8 + (own >> 1),
        jnp.where(
            (own & 3) == 2, 4 + (own >> 2), jnp.where((own & 7) == 4, 2 + (own >> 3), own >> 3)
        ),
    )


def pack_kernel(k_ref, v_ref, lists_ref, slots_ref, *outs):
    slots_ref[...] = slot_of(lists_ref[...])
    for slot, own in enumerate(SLOT_BLOCK):
        for out in outs:
            if slot < out.shape[0]:
                out[slot, 0] = k_ref[own]
                out[slot, 1] = v_ref[own]


def pack(key_blocks, value_blocks, lists, *sizes):
    return pl.pallas_call(
        pack_kernel,
        out_shape=(jax.ShapeDtypeStruct(lists.shape, jnp.int32),)
        + tuple(jax.ShapeDtypeStruct((n, 2, BLOCK, HEAD), jnp.bfloat16) for n in sizes),
        in_specs=[VMEM] * 3,
        out_specs=(VMEM,) * (1 + len(sizes)),
        compiler_params=params(),
        name="pack",
    )(key_blocks, value_blocks, lists)


def hand_on_kernel(*refs):
    count = len(refs) // 2
    for ref, out_ref in zip(refs[:count], refs[count:]):
        out_ref[...] = ref[: out_ref.shape[0]]


def hand_on(values):
    return pl.pallas_call(
        hand_on_kernel,
        out_shape=tuple(
            jax.ShapeDtypeStruct((x.shape[0] // 2,) + x.shape[1:], x.dtype) for x in values
        ),
        in_specs=[VMEM] * len(values),
        out_specs=(VMEM,) * len(values),
        compiler_params=params(),
        name="hand_on",
    )(*values)


def merge_kernel(*refs):
    count = len(refs) // 3
    for base, more, out in zip(refs[:count], refs[count : 2 * count], refs[2 * count :]):
        half = more.shape[0]
        total = base[:half].astype(jnp.float32) + more[...].astype(jnp.float32)
        out[:half] = total.astype(jnp.bfloat16)
        out[half:] = base[half:]


def merge(bases, mores):
    return pl.pallas_call(
        merge_kernel,
        out_shape=tuple(jax.ShapeDtypeStruct(x.shape, x.dtype) for x in bases),
        in_specs=[VMEM] * (2 * len(bases)),
        out_specs=(VMEM,) * len(bases),
        compiler_params=params(),
        name="merge",
    )(*bases, *mores)


def lane_all(x):
    return jnp.broadcast_to(x, (x.shape[0], 128))


def entries_of(group):
    return [
        (n, start + c) for n, (band, side, start, sel, by) in enumerate(group) for c in range(sel)
    ]


def gather(kv, entries, slots, i, which):
    return jnp.concatenate([kv[n][slots[i, c], which] for n, c in entries], axis=0)


def block(e):
    return slice(e * BLOCK, (e + 1) * BLOCK)


def bias_of(bias, entry):
    return bias[entry[0] * 2 + entry[1]]


STAT = jax.ShapeDtypeStruct((NBLK, BLOCK, 128), jnp.float32)
HALF = jax.ShapeDtypeStruct((NBLK, BLOCK, HEAD), jnp.bfloat16)
UNROLL = 4


def staggered(stages, copies=UNROLL):
    for tick in range(copies + len(stages) - 1):
        for n, stage in enumerate(stages):
            if 0 <= tick - n < copies:
                stage(tick - n)


def forward_local_kernel(q_ref, k_ref, v_ref, m_ref, l_ref, acc_ref, *scratch):
    width = NBLK * BLOCK

    def step(t, carry):
        def scores(u):
            scratch[2 * u][...] = nt(q_ref[t * UNROLL + u], k_ref[...].reshape(width, HEAD))

        def weights(u):
            s_ref, p_ref = scratch[2 * u : 2 * u + 2]
            top = s_ref[:, block(0)]
            for e in range(1, NBLK):
                top = jnp.maximum(top, s_ref[:, block(e)])
            m = lane_all(jnp.max(top, axis=1, keepdims=True))
            m_ref[t * UNROLL + u] = m
            total = jnp.zeros((BLOCK, 128), jnp.float32)
            for e in range(NBLK):
                p = jnp.exp2((s_ref[:, block(e)] - m) * COEF)
                total += p
                p_ref[:, block(e)] = p.astype(jnp.bfloat16)
            l_ref[t * UNROLL + u] = total

        def sums(u):
            acc_ref[t * UNROLL + u] = nn(scratch[2 * u + 1][...], v_ref[...].reshape(width, HEAD))

        staggered((scores, weights, sums))
        return carry

    lax.fori_loop(0, NBLK // UNROLL, step, 0)


def forward_scratch(width):
    return [
        pltpu.VMEM((BLOCK, width), jnp.float32),
        pltpu.VMEM((BLOCK, width), jnp.bfloat16),
    ] * UNROLL


def forward_local(q, k, v):
    return pl.pallas_call(
        forward_local_kernel,
        out_shape=(STAT, STAT, STAT),
        in_specs=[VMEM] * 3,
        out_specs=(VMEM,) * 3,
        scratch_shapes=forward_scratch(NBLK * BLOCK),
        compiler_params=params(),
        cost_estimate=cost(256, 2, 1, 5 * MIB),
        name="forward_local",
    )(q, k, v)


def forward_far_kernel(group, last, *refs):
    count = len(group)
    slots, bias, q_ref, mi_ref, li_ref, acci_ref = refs[:6]
    kv = refs[6 : 6 + count]
    rest = refs[6 + count :]
    if last:
        g_ref, out_ref, lse_ref, delta_ref = rest[:4]
        scratch = rest[4:]
    else:
        m_ref, l_ref, acc_ref = rest[:3]
        scratch = rest[3:]
    entries = entries_of(group)

    def step(t, carry):
        highs = [None] * UNROLL
        totals = [None] * UNROLL

        def scores(u):
            i = t * UNROLL + u
            scratch[2 * u][...] = nt(q_ref[i], gather(kv, entries, slots, i, 0))

        def weights(u):
            i = t * UNROLL + u
            s_ref, p_ref = scratch[2 * u : 2 * u + 2]
            top = None
            for n in range(count):
                own = [e for e in range(len(entries)) if entries[e][0] == n]
                part = s_ref[:, block(own[0])]
                for e in own[1:]:
                    part = jnp.maximum(part, s_ref[:, block(e)])
                part = part - bias_of(bias, group[n])
                top = part if top is None else jnp.maximum(top, part)
            m = jnp.maximum(mi_ref[i], lane_all(jnp.max(top, axis=1, keepdims=True)))
            total = li_ref[i] * jnp.exp2((mi_ref[i] - m) * COEF)
            offsets = [m + bias_of(bias, entry) for entry in group]
            for e, (n, c) in enumerate(entries):
                p = jnp.exp2((s_ref[:, block(e)] - offsets[n]) * COEF)
                total += p
                p_ref[:, block(e)] = p.astype(jnp.bfloat16)
            highs[u] = m
            totals[u] = total

        def sums(u):
            i = t * UNROLL + u
            m = highs[u]
            acc = acci_ref[i] * jnp.exp2((mi_ref[i] - m) * COEF)
            acc += nn(scratch[2 * u + 1][...], gather(kv, entries, slots, i, 1))
            if last:
                full = lane_all(jnp.sum(totals[u], axis=1, keepdims=True))
                out = (acc / full).astype(jnp.bfloat16)
                out_ref[i] = out
                lse_ref[i] = m * COEF + jnp.log2(full)
                delta = jnp.sum(
                    g_ref[i].astype(jnp.float32) * out.astype(jnp.float32), axis=1, keepdims=True
                )
                delta_ref[i] = lane_all(delta)
            else:
                m_ref[i] = m
                l_ref[i] = totals[u]
                acc_ref[i] = acc

        staggered((scores, weights, sums))
        return carry

    lax.fori_loop(0, NBLK // UNROLL, step, 0)


def forward_far(group, last, slots, bias, q, stats, kv, grad):
    entries = entries_of(group)
    extra = (grad,) if last else ()
    return pl.pallas_call(
        functools.partial(forward_far_kernel, group, last),
        out_shape=(HALF, STAT, STAT) if last else (STAT, STAT, STAT),
        in_specs=[SMEM, SMEM] + [VMEM] * (4 + len(kv) + len(extra)),
        out_specs=(VMEM,) * 3,
        scratch_shapes=forward_scratch(len(entries) * BLOCK),
        compiler_params=params(),
        cost_estimate=cost(16 * len(entries), 2, 1, 8 * MIB),
        name="forward_far",
    )(slots, bias, q, *stats, *kv, *extra)


def backward_scratch(rows, width, copies):
    return [
        pltpu.VMEM((rows, width), jnp.bfloat16),
        pltpu.VMEM((rows, width), jnp.bfloat16),
    ] * copies


CHUNK = 2


def backward_far_kernel(group, first, *refs):
    count = len(group)
    slots, bias, q_ref, g_ref, lse_ref, delta_ref = refs[:6]
    kv = refs[6 : 6 + count]
    rest = refs[6 + count :]
    if not first:
        dqi_ref, rest = rest[0], rest[1:]
    dq_ref, part, acc = rest[0], rest[1 : 1 + count], rest[1 + count : 1 + 2 * count]
    scratch = rest[1 + 2 * count :]
    entries = entries_of(group)
    for a in acc:
        a[...] = jnp.zeros_like(a)

    def step(t, carry):
        def weights(u):
            i = t * UNROLL + u
            p_ref, ds_ref = scratch[2 * u : 2 * u + 2]
            q = q_ref[i]
            g = g_ref[i]
            lse = lse_ref[i]
            delta = delta_ref[i]
            offsets = [lse + bias_of(bias, entry) for entry in group]
            for e in range(0, len(entries), CHUNK):
                some = entries[e : e + CHUNK]
                s = nt(q, gather(kv, some, slots, i, 0))
                d = nt(g, gather(kv, some, slots, i, 1))
                for f, (n, c) in enumerate(some):
                    p = jnp.exp2(s[:, block(f)] * COEF - offsets[n])
                    p_ref[:, block(e + f)] = p.astype(jnp.bfloat16)
                    ds = p * (d[:, block(f)] - delta)
                    ds_ref[:, block(e + f)] = ds.astype(jnp.bfloat16)

        def sums(u):
            i = t * UNROLL + u
            p_ref, ds_ref = scratch[2 * u : 2 * u + 2]
            dq = nn(ds_ref[...], gather(kv, entries, slots, i, 0))
            dq_ref[i] = dq if first else dq + dqi_ref[i]
            dk = tn(ds_ref[...], q_ref[i])
            dv = tn(p_ref[...], g_ref[i])
            for e, (n, c) in enumerate(entries):
                acc[n][slots[i, c], 0] += dk[block(e)]
                acc[n][slots[i, c], 1] += dv[block(e)]

        staggered((weights, sums))
        return carry

    lax.fori_loop(0, NBLK // UNROLL, step, 0)
    for out, a in zip(part, acc):
        out[...] = a[...].astype(jnp.bfloat16)


def backward_far(group, slots, bias, q, g, lse, delta, kv, dq):
    entries = entries_of(group)
    extra = () if dq is None else (dq,)
    return pl.pallas_call(
        functools.partial(backward_far_kernel, group, dq is None),
        out_shape=(STAT,) + tuple(jax.ShapeDtypeStruct(x.shape, jnp.bfloat16) for x in kv),
        in_specs=[SMEM, SMEM] + [VMEM] * (4 + len(kv) + len(extra)),
        out_specs=(VMEM,) * (1 + len(kv)),
        scratch_shapes=[pltpu.VMEM(x.shape, jnp.float32) for x in kv]
        + backward_scratch(BLOCK, len(entries) * BLOCK, UNROLL),
        compiler_params=params(),
        cost_estimate=cost(16 * len(entries), 5, 1, 8 * MIB),
        name="backward_far",
    )(slots, bias, q, g, lse, delta, *kv, *extra)


LOCAL_ROWS = 2
LOCAL_COPIES = 4


def backward_local_kernel(
    q_ref, g_ref, lse_ref, delta_ref, k_ref, v_ref, dqi_ref, dq_ref, dk_ref, dv_ref, *scratch
):
    rows = LOCAL_ROWS * BLOCK
    width = NBLK * BLOCK
    dk_ref[...] = jnp.zeros_like(dk_ref)
    dv_ref[...] = jnp.zeros_like(dv_ref)

    def step(t, carry):
        def here(ref, u):
            first = (t * LOCAL_COPIES + u) * LOCAL_ROWS
            return ref[pl.ds(first, LOCAL_ROWS)].reshape(rows, 128)

        def weights(u):
            p_ref, ds_ref = scratch[2 * u : 2 * u + 2]
            q = here(q_ref, u)
            g = here(g_ref, u)
            lse = here(lse_ref, u)
            delta = here(delta_ref, u)
            for e in range(0, NBLK, CHUNK):
                s = nt(q, k_ref[e : e + CHUNK].reshape(CHUNK * BLOCK, HEAD))
                d = nt(g, v_ref[e : e + CHUNK].reshape(CHUNK * BLOCK, HEAD))
                for f in range(CHUNK):
                    p = jnp.exp2(s[:, block(f)] * COEF - lse)
                    p_ref[:, block(e + f)] = p.astype(jnp.bfloat16)
                    ds = p * (d[:, block(f)] - delta)
                    ds_ref[:, block(e + f)] = ds.astype(jnp.bfloat16)

        def sums(u):
            p_ref, ds_ref = scratch[2 * u : 2 * u + 2]
            dq = here(dqi_ref, u) + nn(ds_ref[...], k_ref[...].reshape(width, HEAD))
            first = (t * LOCAL_COPIES + u) * LOCAL_ROWS
            dq_ref[pl.ds(first, LOCAL_ROWS)] = (
                (dq * SCALE).astype(jnp.bfloat16).reshape(LOCAL_ROWS, BLOCK, HEAD)
            )
            q = here(q_ref, u)
            g = here(g_ref, u)
            for e in range(NBLK):
                dk_ref[e] += tn(ds_ref[:, block(e)], q)
                dv_ref[e] += tn(p_ref[:, block(e)], g)

        staggered((weights, sums), LOCAL_COPIES)
        return carry

    lax.fori_loop(0, NBLK // (LOCAL_ROWS * LOCAL_COPIES), step, 0)


def backward_local(q, g, lse, delta, k, v, dq):
    return pl.pallas_call(
        backward_local_kernel,
        out_shape=(HALF, STAT, STAT),
        in_specs=[VMEM] * 7,
        out_specs=(VMEM,) * 3,
        scratch_shapes=backward_scratch(LOCAL_ROWS * BLOCK, NBLK * BLOCK, LOCAL_COPIES),
        compiler_params=params(),
        cost_estimate=cost(256, 5, 1, 8 * MIB),
        name="backward_local",
    )(q, g, lse, delta, k, v, dq)


def finish_kernel(dk_ref, dv_ref, *refs):
    parts, (gk_ref, gv_ref) = refs[:-2], refs[-2:]
    for slot, own in enumerate(SLOT_BLOCK):
        dk = dk_ref[own]
        dv = dv_ref[own]
        for part in parts:
            if slot < part.shape[0]:
                dk += part[slot, 0].astype(jnp.float32)
                dv += part[slot, 1].astype(jnp.float32)
        gk_ref[own] = (dk * SCALE).astype(jnp.bfloat16)
        gv_ref[own] = dv.astype(jnp.bfloat16)


def finish(dk, dv, parts):
    return pl.pallas_call(
        finish_kernel,
        out_shape=(HALF, HALF),
        in_specs=[VMEM] * (2 + len(parts)),
        out_specs=(VMEM,) * 2,
        compiler_params=params(),
        name="finish",
    )(dk, dv, *parts)


def local(queries, keys, values, grad_out, block_lists):
    shape = (NBLK, BLOCK, HEAD)
    q, k, v, g = (x.reshape(shape) for x in (queries, keys, values, grad_out))
    position = lax.axis_index("seq")
    devices = lax.axis_size("seq")
    biases = [jnp.float32(0.0)] * 2
    for band, side, start, sel, by in PLAN:
        source = position - by
        valid = jnp.logical_and(source >= 0, source < devices)
        biases.append(jnp.where(valid, 0.0, BIG).astype(jnp.float32))
    bias = jnp.stack(biases)
    fetched = {}

    def fetch(sent, bands):
        for band, side, start, sel, by in PLAN:
            if band in bands:
                fetched[band, side] = shift(sent[band], by)

    def group(*bands):
        chosen = [e for e in PLAN if e[0] in bands]
        return chosen, [fetched[e[0], e[1]] for e in chosen]

    def hold(values, *bands):
        keys_of = [(e[0], e[1]) for e in group(*bands)[0]]
        values, got = lax.optimization_barrier((values, [fetched[x] for x in keys_of]))
        fetched.update(zip(keys_of, got))
        return values

    slots, near, next_near, far = pack(k, v, block_lists, NBLK, 4, 2)
    fetch({1: near, 4: far}, (1, 4))
    stats = forward_local(q, k, v)
    stats, next_near = hold((stats, next_near), 1)
    hops = ((1, 0, 1), (1, 1, -1), (3, 0, 4), (3, 1, -4))
    handed = hand_on([fetched[1, 0], fetched[1, 1]])
    for (band, side, by), part in zip(hops, handed):
        fetched[band + 1, side] = shift(part, by)
    fetch({3: next_near}, (3,))
    for bands, last in (((1,), False), ((2, 3, 4), True)):
        chosen, kv = group(*bands)
        stats = forward_far(chosen, last, slots, bias, q, stats, kv, g)
    out, lse, delta = stats

    def back(dq, *bands):
        chosen, kv = group(*bands)
        return backward_far(chosen, slots, bias, q, g, lse, delta, kv, dq)

    dq, *parts = back(None, 2, 4)
    hop = [shift(part, -by) for part, (band, side, by) in zip(parts, hops)]
    returned = []
    for n, band in ((0, 1), (2, 3)):
        dq, *parts = back(dq, band)
        parts, hop = lax.optimization_barrier((parts, hop))
        parts = merge(parts, hop[n : n + 2])
        returned += [
            shift(part, -by) for part, (own, side, by) in zip(parts, hops[n : n + 2])
        ]
    dq, dk, dv = backward_local(q, g, lse, delta, k, v, dq)
    gk, gv = finish(dk, dv, returned)
    flat = (NBLK * BLOCK, HEAD)
    return tuple(x.reshape(flat) for x in (out, dq, gk, gv))


def solution(mesh):
    spec = P(("dp", "seq"), None)
    return jax.shard_map(
        local,
        mesh=mesh,
        in_specs=(spec,) * 5,
        out_specs=(spec,) * 4,
        check_vma=False,
    )
```
